256 devices in a mesh: dp: 32 (over x, y, core), mp: 8 (over z).
Axes of the slice: x: 4, y: 4, z: 8, core: 2. Of those that a mesh axis runs over, the one named last changes fastest.
Arguments:
- queries: bfloat16 [4096, 4096], P('dp', 'mp'), may hold values from -100 to 100
- neighbours: bfloat16 [128, 256, 896], P(None, 'dp'), may hold values from -6 to 6
- targets: int32 [256], P('dp'), may hold values from 0 to 127, as said below
- counts: int32 [32], P('dp'), may hold values from 0 to 8, as said below
- in_weight: bfloat16 [896, 3584], P(None, 'mp'), may hold values from -0.1875 to 0.1875
- out_weight: bfloat16 [3584, 896], P('mp'), may hold values from -0.09375 to 0.09375
- kv_weight: bfloat16 [896, 2, 4096], P(None, None, 'mp'), may hold values from -0.1875 to 0.1875
- d_context: bfloat16 [4096, 4096], P('dp', 'mp'), may hold values from -6 to 6
Outputs:
- context: bfloat16 [4096, 4096], P('dp', 'mp')
- d_queries: bfloat16 [4096, 4096], P('dp', 'mp')
- grad_kv: float32 [896, 2, 4096], P('dp', None, 'mp')
- grad_in: float32 [896, 3584], P('dp', 'mp')
- grad_out: float32 [3584, 896], P('mp', 'dp')
The draws below stay inside these ranges and needn't reach their ends.
Inputs may be any that keep to these rules, and one draw needn't show every extreme that they name: Every block index o * 4 + p (o an owner, p < 4) is the target of exactly one live slot over all holders; at most 1 live slots of one holder target one owner, and some holder reaches 1; targets of slots that are not live are arbitrary. counts sum to 4 times the number of devices along dp.
All inputs are finite; a program needn't handle non-finite values.
Results may differ from the reference program's by a relative error of at most 0.04.
Values may be sent and summed in bfloat16 or wider, within the bound.
No kernel may reach another device: no remote copies, remote signals or barrier semaphores. Data moves between devices by JAX's collectives and lax.ppermute only.
A program may use at most 64 MiB of HBM per device.

```python
import jax
import jax.numpy as jnp
from jax import lax

H = 32
DH = 128
DE = 896
FE = 3584
SPAN = 64
NLEN = 128
CH = 2
HDH = 4096
NB = 4
HOLD = 8
SLOTS = 256
TOKENS = 4096
N_DP = 32
N_MP = 8


def holder_table(key):
    key_order, key_spread, key_owner, key_place, key_dead = jax.random.split(key, 5)
    holder_order = jax.random.permutation(key_order, N_DP)
    spreads = jax.random.randint(key_spread, (N_DP // 2,), 0, NB + 1)
    spreads = spreads.at[0].set(NB)
    first_half = holder_order[0::2]
    second_half = holder_order[1::2]
    load_counts = jnp.zeros((N_DP,), jnp.int32).at[first_half].set(NB + spreads).at[second_half].set(NB - spreads)
    ordered = load_counts[holder_order]
    ordered_starts = jnp.cumsum(ordered) - ordered
    starts = jnp.zeros((N_DP,), jnp.int32).at[holder_order].set(ordered_starts)
    owner_order = jax.random.permutation(key_owner, N_DP)

    def per_owner(owner_key):
        return jax.random.permutation(owner_key, NB)
    position_table = jax.vmap(per_owner)(jax.random.split(key_place, N_DP))
    slot_index = jnp.arange(HOLD, dtype=jnp.int32)
    entry_index = (starts[:, None] + slot_index[None, :]) % (N_DP * NB)
    owner_ids = owner_order[entry_index % N_DP]
    cycle_index = entry_index // N_DP
    position = position_table[owner_ids, cycle_index]
    is_live = slot_index[None, :] < load_counts[:, None]
    dead_targets = jax.random.randint(key_dead, (N_DP, HOLD), 0, N_DP * NB)
    targets = jnp.where(is_live, owner_ids * NB + position, dead_targets)
    return (targets.reshape(-1).astype(jnp.int32), load_counts.astype(jnp.int32))


def draw_targets(key, part):
    targets, load_counts = holder_table(key)
    return targets


def draw_counts(key, part):
    targets, load_counts = holder_table(key)
    return load_counts


def draw_queries(key, part):
    key = jax.random.fold_in(key, 11)
    key_base = jax.random.fold_in(key, 0)
    values = jnp.clip(jax.random.normal(key_base, (TOKENS, HDH), jnp.float32), -6.0, 6.0)
    return values.astype(jnp.bfloat16)


def steps_of(rng, dims, cuts, smallest, largest):
    level = 1.0
    for dim, parts in cuts:
        draws = jax.random.uniform(jax.random.fold_in(jax.random.fold_in(rng, 6), dim), (parts,), jnp.float32, smallest / len(cuts), largest / len(cuts))
        level = level * jnp.repeat(jnp.exp(draws), dims[dim] // parts).reshape((-1,) + (1,) * (len(dims) - 1 - dim))
    return level


def scatter_about(own_key, shape, deviation, reach, shards=(), kind=jnp.bfloat16):
    entries = jax.random.normal(own_key, shape, jnp.float32) * deviation
    if len(shards) > 0:
        entries = steps_of(own_key, shape, shards, -0.22, 0.18) * entries
    return jnp.clip(entries, min=-reach, max=reach).astype(kind)


def setup_inputs(seed: int = 0) -> dict:
    key_list = jax.random.split(jax.random.key(seed), 9)
    return {
        "queries": draw_queries(jax.random.fold_in(key_list[8], 71), 0),
        "neighbours": scatter_about(key_list[1], (NLEN, SLOTS, DE), 1.0, 6.0, ((1, 32),)),
        "targets": draw_targets(jax.random.fold_in(key_list[8], 71), 0),
        "counts": draw_counts(jax.random.fold_in(key_list[8], 71), 0),
        "in_weight": scatter_about(key_list[4], (DE, FE), DE ** -0.5, 0.1875, ((1, 8),)),
        "out_weight": scatter_about(key_list[5], (FE, DE), FE ** -0.5, 0.09375, ((0, 8),)),
        "kv_weight": scatter_about(key_list[6], (DE, 2, HDH), DE ** -0.5, 0.1875, ((2, 8),)),
        "d_context": scatter_about(key_list[7], (TOKENS, HDH), 1.0, 6.0, ((0, 32), (1, 8))),
    }


GELU_C = 0.7978845608028654
GELU_A = 0.044715
EPSILON = 1e-06

def gelu_value(values):
    inner = GELU_C * (values + GELU_A * values * values * values)
    return 0.5 * values * (1.0 + jnp.tanh(inner))

def gelu_slope(values):
    inner = GELU_C * (values + GELU_A * values * values * values)
    tanh_value = jnp.tanh(inner)
    return 0.5 * (1.0 + tanh_value) + 0.5 * values * (1.0 - tanh_value * tanh_value) * GELU_C * (1.0 + 3.0 * GELU_A * values * values)

def rms_normed(rows):
    wide = rows.astype(jnp.float32)
    mean_square = lax.optimization_barrier(jnp.mean(wide * wide, axis=-1, keepdims=True))
    return (wide * lax.rsqrt(mean_square + EPSILON)).astype(jnp.bfloat16)

def to_spans(values, spans):
    length, blocks, columns = values.shape
    heads = columns // DH
    return values.reshape(length, spans, 2, heads, DH).transpose(1, 2, 0, 3, 4).reshape(spans, 2 * length, heads, DH)

def from_spans(values, length):
    spans, keys_len, heads, depth = values.shape
    return values.reshape(spans, 2, length, heads, depth).transpose(2, 0, 1, 3, 4).reshape(length, 2 * spans, heads * depth)

def attend(queries, keys, values, grads):
    scaling = DH ** (-0.5)
    queries_f = queries.astype(jnp.float32)
    keys_f = keys.astype(jnp.float32)
    values_f = values.astype(jnp.float32)
    grads_f = grads.astype(jnp.float32)
    scores = jnp.einsum('cqhd,ckhd->chqk', queries_f, keys_f) * scaling
    peak = lax.optimization_barrier(jnp.max(scores, axis=-1, keepdims=True))
    weights = jnp.exp(scores - peak)
    probs_wide = weights / lax.optimization_barrier(jnp.sum(weights, axis=-1, keepdims=True))
    probs = probs_wide.astype(jnp.bfloat16)
    context = jnp.einsum('chqk,ckhd->cqhd', probs.astype(jnp.float32), values_f).astype(jnp.bfloat16)
    d_probs = jnp.einsum('cqhd,ckhd->chqk', grads_f, values_f)
    d_scores = (probs_wide * (d_probs - lax.optimization_barrier(jnp.sum(d_probs * probs_wide, axis=-1, keepdims=True))) * scaling).astype(jnp.bfloat16)
    d_scores_f = d_scores.astype(jnp.float32)
    d_queries = jnp.einsum('chqk,ckhd->cqhd', d_scores_f, keys_f).astype(jnp.bfloat16)
    d_keys = jnp.einsum('chqk,cqhd->ckhd', d_scores_f, queries_f).astype(jnp.bfloat16)
    d_values = jnp.einsum('chqk,cqhd->ckhd', probs.astype(jnp.float32), grads_f).astype(jnp.bfloat16)
    return (context, d_queries, d_keys, d_values)

def reference(queries, neighbours, targets, counts, in_weight, out_weight, kv_weight, d_context):
    slot_ids = jnp.arange(SLOTS, dtype=jnp.int32)
    is_live = slot_ids % HOLD < counts[slot_ids // HOLD]
    landing = jnp.where(is_live, targets, N_DP * NB).astype(jnp.int32)
    source = jnp.zeros((N_DP * NB + 1,), jnp.int32).at[landing].set(slot_ids)[:N_DP * NB]
    raw_all = jnp.take(neighbours, source, axis=1).reshape(NLEN, N_DP, NB, DE).transpose(1, 0, 2, 3)
    queries_all = queries.reshape(N_DP, CH * SPAN, HDH)
    grads_all = d_context.reshape(N_DP, CH * SPAN, HDH)
    fe_block = FE // N_MP
    hd_block = HDH // N_MP
    out_blocks = out_weight.astype(jnp.float32).reshape(N_MP, fe_block, DE)
    kv_blocks = kv_weight.astype(jnp.float32).reshape(DE, 2, N_MP, hd_block)

    def owner_step(carry, inputs):
        in_total, out_total, kv_total = carry
        raw, owner_queries, owner_grads = inputs
        normed = rms_normed(raw).reshape(NLEN * NB, DE)
        hidden_pre = jnp.dot(normed, in_weight, preferred_element_type=jnp.float32)
        activated = gelu_value(hidden_pre).astype(jnp.bfloat16)
        partials = jnp.einsum('nmf,mfe->nme', activated.astype(jnp.float32).reshape(NLEN * NB, N_MP, fe_block), out_blocks)
        partials = lax.optimization_barrier(partials.astype(jnp.bfloat16)).astype(jnp.float32)
        encoded = (raw.astype(jnp.float32).reshape(NLEN * NB, DE) + lax.optimization_barrier(jnp.sum(partials, axis=1))).astype(jnp.bfloat16)
        keyvals = jnp.einsum('ne,ejx->njx', encoded.astype(jnp.float32), kv_weight.astype(jnp.float32)).astype(jnp.bfloat16)
        keyvals = keyvals.reshape(NLEN, NB, 2, HDH)
        heads_queries = owner_queries.reshape(CH, SPAN, H, DH)
        heads_grads = owner_grads.reshape(CH, SPAN, H, DH)
        context, d_queries, d_keys, d_values = attend(heads_queries, to_spans(keyvals[:, :, 0], CH), to_spans(keyvals[:, :, 1], CH), heads_grads)
        d_keyvals = jnp.stack([from_spans(d_keys, NLEN), from_spans(d_values, NLEN)], axis=2)
        flat_dkv = d_keyvals.reshape(NLEN * NB, 2, N_MP, hd_block).astype(jnp.float32)
        back_parts = jnp.einsum('njmx,ejmx->nme', flat_dkv, kv_blocks)
        back_parts = lax.optimization_barrier(back_parts.astype(jnp.bfloat16)).astype(jnp.float32)
        d_encoded = lax.optimization_barrier(jnp.sum(back_parts, axis=1)).astype(jnp.bfloat16)
        kv_total = kv_total + jnp.einsum('ne,njx->ejx', encoded.astype(jnp.float32), d_keyvals.reshape(NLEN * NB, 2, HDH).astype(jnp.float32))
        d_act = jnp.dot(d_encoded, out_weight.T, preferred_element_type=jnp.float32)
        d_pre = (d_act * gelu_slope(hidden_pre)).astype(jnp.bfloat16)
        in_total = in_total + jnp.dot(normed.T, d_pre, preferred_element_type=jnp.float32)
        out_total = out_total + jnp.dot(activated.T, d_encoded, preferred_element_type=jnp.float32)
        return ((in_total, out_total, kv_total), (context.reshape(CH * SPAN, HDH), d_queries.reshape(CH * SPAN, HDH)))
    start = (jnp.zeros((DE, FE), jnp.float32), jnp.zeros((FE, DE), jnp.float32), jnp.zeros((DE, 2, HDH), jnp.float32))
    totals, outputs = lax.scan(owner_step, start, (raw_all, queries_all, grads_all))
    grad_in, grad_out, grad_kv = totals
    context_all, d_queries_all = outputs
    return (context_all.reshape(TOKENS, HDH), d_queries_all.reshape(TOKENS, HDH), grad_kv, grad_in, grad_out)
```

```python
import functools

import jax
import jax.numpy as jnp
from jax import lax
from jax.experimental import pallas as pl
from jax.experimental.pallas import tpu as pltpu
from jax.sharding import PartitionSpec as P

DH = 128
SPAN = 64
NEIGH = 2
PLACE = 128
CHUNKS = 2
VMEM_LIMIT = 48 * 1024 * 1024

GELU_C = 0.7978845608028654
GELU_A = 0.044715
EPSILON = 1e-06

BF = jnp.bfloat16
F32 = jnp.float32


def dot_nn(a, b):
    return lax.dot_general(a, b, (((1,), (0,)), ((), ())), preferred_element_type=F32)


def dot_nt(a, b):
    return lax.dot_general(a, b, (((1,), (1,)), ((), ())), preferred_element_type=F32)


def dot_tn(a, b):
    return lax.dot_general(a, b, (((0,), (0,)), ((), ())), preferred_element_type=F32)


def call(kernel, outs, *args, scratch=(), flops=0):
    moved = sum(a.size * a.dtype.itemsize for a in args)
    moved += sum(o.size * o.dtype.itemsize for o in outs)
    return pl.pallas_call(
        kernel,
        out_shape=outs,
        scratch_shapes=list(scratch),
        compiler_params=pltpu.CompilerParams(vmem_limit_bytes=VMEM_LIMIT),
        cost_estimate=pl.CostEstimate(flops=flops, bytes_accessed=moved, transcendentals=0),
    )(*args)


def shape_of(shape, dtype=BF):
    return jax.ShapeDtypeStruct(shape, dtype)


def place_kernel(tokens, blocks, got_ref, raw_ref):
    rows, width = got_ref.shape
    wide = width - PLACE
    marks = got_ref[:, wide:]
    spread_rows = lax.broadcasted_iota(jnp.int32, (PLACE, blocks * tokens), 0)
    spread_cols = lax.broadcasted_iota(jnp.int32, (PLACE, blocks * tokens), 1)
    spread = (spread_rows == spread_cols // tokens).astype(BF)
    chosen = dot_nn(marks, spread)
    row_token = lax.broadcasted_iota(jnp.int32, chosen.shape, 0) % tokens
    col_token = lax.broadcasted_iota(jnp.int32, chosen.shape, 1) % tokens
    chosen = jnp.where(row_token == col_token, chosen, 0.0).astype(BF)
    raw_ref[...] = dot_tn(chosen, got_ref[:, :wide]).astype(BF)


def encode_kernel(raw_ref, win_ref, wout_ref, normed_ref, act_ref, slope_ref, part_ref):
    wide = raw_ref[...].astype(F32)
    mean_square = jnp.mean(wide * wide, axis=-1, keepdims=True)
    normed = (wide * lax.rsqrt(mean_square + EPSILON)).astype(BF)
    normed_ref[...] = normed
    pre = dot_nn(normed, win_ref[...])
    square = pre * pre
    tanh_value = jnp.tanh(GELU_C * (pre + GELU_A * square * pre))
    act = (0.5 * pre * (1.0 + tanh_value)).astype(BF)
    act_ref[...] = act
    slope = 0.5 * (1.0 + tanh_value) + 0.5 * pre * (1.0 - tanh_value * tanh_value) * GELU_C * (
        1.0 + 3.0 * GELU_A * square
    )
    slope_ref[...] = slope.astype(BF)
    part_ref[...] = dot_nn(act, wout_ref[...]).astype(BF)


def attend_kernel(spans, enc_ref, kw_ref, vw_ref, q_ref, g_ref, ctx_ref, dq_ref, dk_ref, dv_ref, part_ref):
    scaling = DH ** (-0.5)
    rows = enc_ref.shape[0] // spans
    enc = enc_ref[...]
    keys = dot_nn(enc, kw_ref[...]).astype(BF)
    values = dot_nn(enc, vw_ref[...]).astype(BF)
    heads = keys.shape[1] // DH
    for s in range(spans):
        key_rows = slice(s * rows, (s + 1) * rows)
        q_rows = slice(s * SPAN, (s + 1) * SPAN)
        for h in range(heads):
            cols = slice(h * DH, (h + 1) * DH)
            k = keys[key_rows, cols]
            v = values[key_rows, cols]
            q = q_ref[q_rows, cols]
            g = g_ref[q_rows, cols]
            scores = dot_nt(q, k) * scaling
            peak = jnp.max(scores, axis=-1, keepdims=True)
            weights = jnp.exp(scores - peak)
            probs_wide = weights / jnp.sum(weights, axis=-1, keepdims=True)
            probs = probs_wide.astype(BF)
            ctx_ref[q_rows, cols] = dot_nn(probs, v).astype(BF)
            d_probs = dot_nt(g, v)
            inner = jnp.sum(d_probs * probs_wide, axis=-1, keepdims=True)
            d_scores = (probs_wide * (d_probs - inner) * scaling).astype(BF)
            dq_ref[q_rows, cols] = dot_nn(d_scores, k).astype(BF)
            dk_ref[key_rows, cols] = dot_tn(d_scores, q).astype(BF)
            dv_ref[key_rows, cols] = dot_tn(probs, g).astype(BF)
    part_ref[...] = (dot_nt(dk_ref[...], kw_ref[...]) + dot_nt(dv_ref[...], vw_ref[...])).astype(BF)


def kv_grad_kernel(chunks, *refs):
    encs, dks, dvs = refs[:chunks], refs[chunks : 2 * chunks], refs[2 * chunks : 3 * chunks]
    k_ref, v_ref = refs[3 * chunks :]
    k_ref[...] = sum(dot_tn(e[...], d[...]) for e, d in zip(encs, dks)).astype(BF)
    v_ref[...] = sum(dot_tn(e[...], d[...]) for e, d in zip(encs, dvs)).astype(BF)


def out_grad_kernel(chunks, *refs):
    d_encs, acts = refs[:chunks], refs[chunks : 2 * chunks]
    refs[-1][...] = sum(dot_tn(d[...], a[...]) for d, a in zip(d_encs, acts)).astype(BF)


def in_grad_kernel(chunks, *refs):
    d_encs, normeds, slopes = refs[:chunks], refs[chunks : 2 * chunks], refs[2 * chunks : 3 * chunks]
    wout_ref, total_ref = refs[3 * chunks :]
    total = 0.0
    for d, n, s in zip(d_encs, normeds, slopes):
        d_pre = (dot_nt(d[...], wout_ref[...]) * s[...].astype(F32)).astype(BF)
        total = total + dot_tn(n[...], d_pre)
    total_ref[...] = total.astype(BF)


def gather_mp(piece, ranks):
    rows, width = piece.shape
    copies = jnp.broadcast_to(piece[None], (ranks, rows, width))
    return lax.all_to_all(copies, "mp", 0, 0, tiled=True).reshape(ranks * rows, width)


def scatter_mp(parts, ranks):
    rows, width = parts.shape
    got = lax.all_to_all(parts.reshape(ranks, rows // ranks, width), "mp", 0, 0, tiled=True)
    return jnp.sum(got.astype(F32), axis=0)


def scatter_dp(total, devices):
    rows, width = total.shape
    chips = devices // 2
    core = lax.axis_index("dp") % 2
    split = total.reshape(chips, 2, rows // devices, width)
    give = lax.dynamic_index_in_dim(split, 1 - core, 1, keepdims=False)
    keep = lax.dynamic_index_in_dim(split, core, 1, keepdims=False)
    got = lax.ppermute(give, "dp", [(i, i ^ 1) for i in range(devices)])
    pair = (keep.astype(F32) + got.astype(F32)).astype(BF)
    groups = [[chip * 2 + c for chip in range(chips)] for c in range(2)]
    every = lax.all_to_all(pair, "dp", 0, 0, axis_index_groups=groups, tiled=True)
    return jnp.sum(every.astype(F32), axis=0)


def per_device(queries, neighbours, targets, counts, in_weight, out_weight, kv_weight, d_context):
    length, holding, width = neighbours.shape
    owners = lax.axis_size("dp")
    ranks = lax.axis_size("mp")
    tokens = length // ranks
    token_rows, columns = queries.shape
    hidden = in_weight.shape[1]
    spans = token_rows // SPAN
    blocks = NEIGH * spans
    my_rank = lax.axis_index("mp")

    own = lax.dynamic_slice_in_dim(neighbours, my_rank * tokens, tokens, 0).reshape(tokens * holding, width)
    is_live = jnp.arange(holding, dtype=jnp.int32) < counts[0]
    dest = jnp.where(is_live, targets // blocks, -1)
    place = targets % blocks
    marks = jnp.arange(PLACE, dtype=jnp.int32)[None, :] == jnp.tile(place, tokens)[:, None]
    payload = jnp.concatenate([own, marks.astype(BF)], axis=1)
    row_ids = jnp.arange(owners * tokens, dtype=jnp.int32)
    col_ids = jnp.arange(tokens * holding, dtype=jnp.int32)
    pick = jnp.logical_and(
        (row_ids // tokens)[:, None] == jnp.tile(dest, tokens)[None, :],
        (row_ids % tokens)[:, None] == (col_ids // holding)[None, :],
    ).astype(BF)
    sent = dot_nn(pick, payload).astype(BF).reshape(owners, tokens, width + PLACE)
    got = lax.all_to_all(sent, "dp", 0, 0, tiled=True).reshape(owners * tokens, width + PLACE)
    (raw,) = call(
        functools.partial(place_kernel, tokens, blocks),
        [shape_of((blocks * tokens, width))],
        got,
        flops=2 * owners * tokens * blocks * tokens * width,
    )

    kw = kv_weight[:, 0, :]
    vw = kv_weight[:, 1, :]

    per_chunk = spans // CHUNKS
    piece_rows = blocks * tokens // CHUNKS
    chunk_rows = piece_rows * ranks
    raws = [raw[c * piece_rows : (c + 1) * piece_rows] for c in range(CHUNKS)]
    kept = []
    parts = []
    for c in range(CHUNKS):
        every = gather_mp(raws[c], ranks)
        if per_chunk > 1:
            every = (
                every.reshape(ranks, per_chunk, -1, width).transpose(1, 0, 2, 3).reshape(chunk_rows, width)
            )
        normed, act, slope, part = call(
            encode_kernel,
            [
                shape_of((chunk_rows, width)),
                shape_of((chunk_rows, hidden)),
                shape_of((chunk_rows, hidden)),
                shape_of((chunk_rows, width)),
            ],
            every,
            in_weight,
            out_weight,
            flops=4 * chunk_rows * width * hidden,
        )
        kept.append((normed, act, slope))
        parts.append(part)
    pieces = []
    for c in range(CHUNKS):
        part = parts[c]
        summed = scatter_mp(part, ranks)
        pieces.append((raws[c].astype(F32) + summed).astype(BF))
    encs = [gather_mp(p, ranks) for p in pieces]
    results = []
    for c in range(CHUNKS):
        q_rows = slice(c * per_chunk * SPAN, (c + 1) * per_chunk * SPAN)
        results.append(
            call(
                functools.partial(attend_kernel, per_chunk),
                [
                    shape_of((per_chunk * SPAN, columns)),
                    shape_of((per_chunk * SPAN, columns)),
                    shape_of((chunk_rows, columns)),
                    shape_of((chunk_rows, columns)),
                    shape_of((chunk_rows, width)),
                ],
                encs[c],
                kw,
                vw,
                queries[q_rows],
                d_context[q_rows],
                flops=8 * chunk_rows * width * columns,
            )
        )
    d_encs = [gather_mp(scatter_mp(r[4], ranks).astype(BF), ranks) for r in results]
    kv_k, kv_v = call(
        functools.partial(kv_grad_kernel, CHUNKS),
        [shape_of((width, columns))] * 2,
        *encs,
        *[r[2] for r in results],
        *[r[3] for r in results],
        flops=4 * CHUNKS * chunk_rows * width * columns,
    )
    grad_kv = scatter_dp(jnp.concatenate([kv_k, kv_v], axis=1), owners)
    (out_total,) = call(
        functools.partial(out_grad_kernel, CHUNKS),
        [shape_of((width, hidden))],
        *d_encs,
        *[k[1] for k in kept],
        flops=2 * CHUNKS * chunk_rows * width * hidden,
    )
    grad_out_t = scatter_dp(out_total, owners)
    (in_total,) = call(
        functools.partial(in_grad_kernel, CHUNKS),
        [shape_of((width, hidden))],
        *d_encs,
        *[k[0] for k in kept],
        *[k[2] for k in kept],
        out_weight,
        flops=4 * CHUNKS * chunk_rows * width * hidden,
    )
    grad_in = scatter_dp(in_total, owners)
    context = jnp.concatenate([r[0] for r in results], axis=0)
    d_queries = jnp.concatenate([r[1] for r in results], axis=0)
    return (
        context,
        d_queries,
        grad_kv.reshape(width // owners, 2, columns),
        grad_in,
        grad_out_t.T,
    )


def solution(mesh):
    placed = (
        P("dp", "mp"),
        P(None, "dp", None),
        P("dp"),
        P("dp"),
        P(None, "mp"),
        P("mp", None),
        P(None, None, "mp"),
        P("dp", "mp"),
    )
    return jax.shard_map(
        per_device,
        mesh=mesh,
        in_specs=placed,
        out_specs=(P("dp", "mp"), P("dp", "mp"), P("dp", None, "mp"), P("dp", "mp"), P("mp", "dp")),
        check_vma=False,
    )
```

```python
import functools

import jax
import jax.numpy as jnp
from jax import lax
from jax.experimental import pallas as pl
from jax.experimental.pallas import tpu as pltpu
from jax.sharding import PartitionSpec as P

DH = 128
SPAN = 64
NEIGH = 2
PLACE = 128
OFFSETS = (0, 1, 3, -1, -3, 2, -2, 4)
VMEM_LIMIT = 24 * 1024 * 1024

GELU_C = 0.7978845608028654
GELU_A = 0.044715
EPSILON = 1e-06

BF = jnp.bfloat16
F32 = jnp.float32


def dot_nn(a, b):
    return lax.dot_general(a, b, (((1,), (0,)), ((), ())), preferred_element_type=F32)


def dot_nt(a, b):
    return lax.dot_general(a, b, (((1,), (1,)), ((), ())), preferred_element_type=F32)


def dot_tn(a, b):
    return lax.dot_general(a, b, (((0,), (0,)), ((), ())), preferred_element_type=F32)


def call(kernel, outs, *args, scratch=(), flops=0, smem=0):
    moved = sum(a.size * a.dtype.itemsize for a in args)
    moved += sum(o.size * o.dtype.itemsize for o in outs)
    whole = pl.BlockSpec(memory_space=pltpu.VMEM)
    scalar = pl.BlockSpec(memory_space=pltpu.SMEM)
    return pl.pallas_call(
        kernel,
        out_shape=outs,
        in_specs=[scalar] * smem + [whole] * (len(args) - smem),
        out_specs=[whole] * len(outs),
        scratch_shapes=list(scratch),
        compiler_params=pltpu.CompilerParams(vmem_limit_bytes=VMEM_LIMIT),
        cost_estimate=pl.CostEstimate(flops=flops, bytes_accessed=moved, transcendentals=0),
    )(*args)


def shape_of(shape, dtype=BF):
    return jax.ShapeDtypeStruct(shape, dtype)


def place_kernel(tokens, blocks, got_ref, raw_ref):
    rows, width = got_ref.shape
    wide = width - PLACE
    marks = got_ref[:, wide:]
    spread_rows = lax.broadcasted_iota(jnp.int32, (PLACE, blocks * tokens), 0)
    spread_cols = lax.broadcasted_iota(jnp.int32, (PLACE, blocks * tokens), 1)
    spread = (spread_rows == spread_cols // tokens).astype(BF)
    chosen = dot_nn(marks, spread)
    row_token = lax.broadcasted_iota(jnp.int32, chosen.shape, 0) % tokens
    col_token = lax.broadcasted_iota(jnp.int32, chosen.shape, 1) % tokens
    chosen = jnp.where(row_token == col_token, chosen, 0.0).astype(BF)
    raw_ref[...] = dot_tn(chosen, got_ref[:, :wide]).astype(BF)


def join(refs):
    own, p1, p3, m1, m3, p2, m2, low, high = refs
    return jnp.concatenate([r[...] for r in (own, p1, p3, m1, m3, p2, m2, low, high)], axis=0)


def part_shapes(piece, width):
    rows = (piece, 2 * piece, 2 * piece, piece, piece, piece // 2, piece // 2)
    return [shape_of((r, width)) for r in rows]


def write_parts(part, refs):
    at = 0
    for ref in refs:
        rows = ref.shape[0]
        ref[...] = part[at : at + rows]
        at += rows


def relay_kernel(ahead_ref, behind_ref, low_ref, high_ref, p2_ref, m2_ref, p2_out, m2_out):
    piece = p2_ref.shape[0]
    half = piece // 2
    plus = p2_ref[...].astype(F32) + ahead_ref[piece:].astype(F32)
    minus = m2_ref[...].astype(F32) + behind_ref[piece:].astype(F32)
    p2_out[:half] = (plus[:half] + low_ref[...].astype(F32)).astype(BF)
    p2_out[half:] = plus[half:].astype(BF)
    m2_out[:half] = minus[:half].astype(BF)
    m2_out[half:] = (minus[half:] + high_ref[...].astype(F32)).astype(BF)


def sum_kernel(*refs):
    own_ref, ahead_ref, behind_ref, p2_ref, m2_ref = refs[:5]
    piece = own_ref.shape[0]
    total = own_ref[...].astype(F32) + ahead_ref[:piece].astype(F32) + behind_ref[:piece].astype(F32)
    total = total + p2_ref[...].astype(F32) + m2_ref[...].astype(F32)
    for extra in refs[5:-1]:
        total = total + extra[...].astype(F32)
    refs[-1][...] = total.astype(BF)


def shift(array, hops, ranks):
    return lax.ppermute(array, "mp", [(i, (i + hops) % ranks) for i in range(ranks)])


def gather_ring(piece, ranks):
    half = piece.shape[0] // 2
    p1, m1 = shift(piece, -1, ranks), shift(piece, 1, ranks)
    p2, m2 = shift(piece, -2, ranks), shift(piece, 2, ranks)
    p3, m3 = shift(p2, -1, ranks), shift(m2, 1, ranks)
    low, high = shift(p2[:half], -2, ranks), shift(m2[half:], 2, ranks)
    return (piece, p1, p3, m1, m3, p2, m2, low, high)


def scatter_ring(parts, ranks, *extra):
    own, ahead, behind, p2, m2, low, high = parts
    ahead, behind = shift(ahead, 1, ranks), shift(behind, -1, ranks)
    low, high = shift(low, 2, ranks), shift(high, -2, ranks)
    p2, m2 = call(
        relay_kernel,
        [shape_of(p2.shape)] * 2,
        ahead,
        behind,
        low,
        high,
        p2,
        m2,
    )
    p2, m2 = shift(p2, 2, ranks), shift(m2, -2, ranks)
    (total,) = call(sum_kernel, [shape_of(own.shape)], own, ahead, behind, p2, m2, *extra)
    return total


def encode_kernel(*refs):
    win_ref, wout_ref, normed_ref, act_ref, slope_ref = refs[9:14]
    wide = join(refs[:9]).astype(F32)
    mean_square = jnp.mean(wide * wide, axis=-1, keepdims=True)
    normed = (wide * lax.rsqrt(mean_square + EPSILON)).astype(BF)
    normed_ref[...] = normed
    pre = dot_nt(normed, win_ref[...])
    square = pre * pre
    tanh_value = jnp.tanh(GELU_C * (pre + GELU_A * square * pre))
    act = (0.5 * pre * (1.0 + tanh_value)).astype(BF)
    act_ref[...] = act
    slope = 0.5 * (1.0 + tanh_value) + 0.5 * pre * (1.0 - tanh_value * tanh_value) * GELU_C * (
        1.0 + 3.0 * GELU_A * square
    )
    slope_ref[...] = slope.astype(BF)
    write_parts(dot_nn(act, wout_ref[...]).astype(BF), refs[14:])


def deal(core, total_ref, keep_ref, give_ref, cols, slot_of):
    chips = keep_ref.shape[0]
    rows = total_ref.shape[0] // (2 * chips)
    filler = jnp.zeros((keep_ref.shape[1] - rows, total_ref.shape[1]), BF)

    def write(first, second):
        for chip in range(chips):
            at = 2 * chip * rows
            slot = slot_of(chip)
            first[slot, :rows, cols] = total_ref[at : at + rows, :].astype(BF)
            second[slot, :rows, cols] = total_ref[at + rows : at + 2 * rows, :].astype(BF)
            if filler.shape[0]:
                first[slot, rows:, cols] = filler
                second[slot, rows:, cols] = filler

    @pl.when(core == 0)
    def _():
        write(keep_ref, give_ref)

    @pl.when(core != 0)
    def _():
        write(give_ref, keep_ref)


def attend_kernel(spans, ranks, *refs):
    kw_ref, vw_ref, q_ref, g_ref, ctx_ref, dq_ref, enc_ref, dk_ref, dv_ref = refs[9:18]
    scaling = DH ** (-0.5)
    enc = join(refs[:9])
    enc_ref[...] = enc
    rows, columns = dk_ref.shape
    piece = rows // ranks // spans
    cut = (ranks, spans, piece, columns)
    keys = dot_nn(enc, kw_ref[...]).astype(BF).reshape(cut)
    values = dot_nn(enc, vw_ref[...]).astype(BF).reshape(cut)
    for s in range(spans):
        q_rows = slice(s * SPAN, (s + 1) * SPAN)
        for h in range(columns // DH):
            cols = slice(h * DH, (h + 1) * DH)
            k = keys[:, s, :, cols].reshape(ranks * piece, DH)
            v = values[:, s, :, cols].reshape(ranks * piece, DH)
            q = q_ref[q_rows, cols]
            g = g_ref[q_rows, cols]
            scores = dot_nt(q, k) * scaling
            peak = jnp.max(scores, axis=-1, keepdims=True)
            weights = jnp.exp(scores - peak)
            probs_wide = weights / jnp.sum(weights, axis=-1, keepdims=True)
            probs = probs_wide.astype(BF)
            ctx_ref[q_rows, cols] = dot_nn(probs, v).astype(BF)
            d_probs = dot_nt(g, v)
            inner = jnp.sum(d_probs * probs_wide, axis=-1, keepdims=True)
            d_scores = (probs_wide * (d_probs - inner) * scaling).astype(BF)
            dq_ref[q_rows, cols] = dot_nn(d_scores, k).astype(BF)
            d_k = dot_tn(d_scores, q).astype(BF)
            d_v = dot_tn(probs, g).astype(BF)
            for r in range(ranks):
                at = (r * spans + s) * piece
                dk_ref[at : at + piece, cols] = d_k[r * piece : (r + 1) * piece]
                dv_ref[at : at + piece, cols] = d_v[r * piece : (r + 1) * piece]
    part = (dot_nt(dk_ref[...], kw_ref[...]) + dot_nt(dv_ref[...], vw_ref[...])).astype(BF)
    write_parts(part, refs[18:])


def kv_grads_kernel(sides, at_ref, enc_ref, dk_ref, dv_ref, keep_ref, give_ref, total_ref):
    columns = dk_ref.shape[1]

    def slot_of(chip):
        x, y = chip // sides[1], chip % sides[1]
        ahead = lax.rem(x - at_ref[1] + sides[0], sides[0])
        beside = lax.rem(y - at_ref[2] + sides[1], sides[1])
        return ahead * sides[1] + beside

    enc = enc_ref[...]
    total_ref[...] = dot_tn(enc, dk_ref[...])
    deal(at_ref[0], total_ref, keep_ref, give_ref, slice(0, columns), slot_of)
    total_ref[...] = dot_tn(enc, dv_ref[...])
    deal(at_ref[0], total_ref, keep_ref, give_ref, slice(columns, 2 * columns), slot_of)


def grads_kernel(*refs):
    at_ref, normed_ref, act_ref, slope_ref, wout_ref, keep_ref, give_ref, total_ref = refs[:1] + refs[10:]
    hidden = act_ref.shape[1]
    d_enc = join(refs[1:10])
    total_ref[...] = dot_tn(d_enc, act_ref[...])
    deal(at_ref[0], total_ref, keep_ref, give_ref, slice(0, hidden), lambda chip: chip)
    d_pre = (dot_nt(d_enc, wout_ref[...]) * slope_ref[...].astype(F32)).astype(BF)
    total_ref[...] = dot_tn(normed_ref[...], d_pre)
    deal(at_ref[0], total_ref, keep_ref, give_ref, slice(hidden, 2 * hidden), lambda chip: chip)


def swap_cores(give, devices):
    return lax.ppermute(give, "dp", [(i, i ^ 1) for i in range(devices)])


def scatter_chips(pair, devices):
    chips = devices // 2
    groups = [[chip * 2 + c for chip in range(chips)] for c in range(2)]
    every = lax.all_to_all(pair, "dp", 0, 0, axis_index_groups=groups, tiled=True)
    return jnp.sum(every.astype(F32), axis=0)


def scatter_axis(pieces, size, stride, devices):
    total = pieces[0].astype(F32)
    for k in range(1, size):
        perm = []
        for i in range(devices):
            at = i // stride % size
            perm.append((i, i + ((at + k) % size - at) * stride))
        total = total + lax.ppermute(pieces[k], "dp", perm).astype(F32)
    return total


def scatter_two_axes(keep, give, sides, devices):
    got = swap_cores(give, devices)
    across, beside = sides
    cut = (across, beside) + keep.shape[1:]
    keep, got = keep.reshape(cut), got.reshape(cut)
    pieces = [(keep[k].astype(F32) + got[k].astype(F32)).astype(BF) for k in range(across)]
    half = scatter_axis(pieces, across, 2 * beside, devices).astype(BF)
    return scatter_axis([half[k] for k in range(beside)], beside, 2, devices)


def per_device(queries, neighbours, targets, counts, in_weight, out_weight, kv_weight, d_context):
    length, holding, width = neighbours.shape
    owners = lax.axis_size("dp")
    ranks = lax.axis_size("mp")
    tokens = length // ranks
    token_rows, columns = queries.shape
    hidden = in_weight.shape[1]
    spans = token_rows // SPAN
    blocks = NEIGH * spans
    my_rank = lax.axis_index("mp")
    me = lax.axis_index("dp")
    across = 1
    while across * across < owners // 2:
        across *= 2
    sides = (across, owners // 2 // across)
    at = jnp.stack([me % 2, me // 2 // sides[1], me // 2 % sides[1]]).astype(jnp.int32)
    piece = blocks * tokens
    rows = ranks * piece
    chips = owners // 2
    out_rows = width // owners
    pad_rows = -(-out_rows // 16) * 16

    own = lax.dynamic_slice_in_dim(neighbours, my_rank * tokens, tokens, 0).reshape(tokens * holding, width)
    is_live = jnp.arange(holding, dtype=jnp.int32) < counts[0]
    dest = jnp.where(is_live, targets // blocks, -1)
    place = targets % blocks
    marks = jnp.arange(PLACE, dtype=jnp.int32)[None, :] == jnp.tile(place, tokens)[:, None]
    payload = jnp.concatenate([own, marks.astype(BF)], axis=1)
    row_ids = jnp.arange(owners * tokens, dtype=jnp.int32)
    col_ids = jnp.arange(tokens * holding, dtype=jnp.int32)
    pick = jnp.logical_and(
        (row_ids // tokens)[:, None] == jnp.tile(dest, tokens)[None, :],
        (row_ids % tokens)[:, None] == (col_ids // holding)[None, :],
    ).astype(BF)
    sent = dot_nn(pick, payload).astype(BF).reshape(owners, tokens, width + PLACE)
    got = lax.all_to_all(sent, "dp", 0, 0, tiled=True).reshape(owners * tokens, width + PLACE)
    (raw,) = call(
        functools.partial(place_kernel, tokens, blocks),
        [shape_of((piece, width))],
        got,
        flops=2 * owners * tokens * piece * width,
    )
    normed, act, slope, *parts = call(
        encode_kernel,
        [
            shape_of((rows, width)),
            shape_of((rows, hidden)),
            shape_of((rows, hidden)),
            *part_shapes(piece, width),
        ],
        *gather_ring(raw, ranks),
        in_weight.T,
        out_weight,
        flops=4 * rows * width * hidden,
    )
    encoded = scatter_ring(parts, ranks, raw)
    context, d_queries, enc, dk, dv, *parts = call(
        functools.partial(attend_kernel, spans, ranks),
        [
            shape_of((token_rows, columns)),
            shape_of((token_rows, columns)),
            shape_of((rows, width)),
            shape_of((rows, columns)),
            shape_of((rows, columns)),
            *part_shapes(piece, width),
        ],
        *gather_ring(encoded, ranks),
        kv_weight[:, 0, :],
        kv_weight[:, 1, :],
        queries,
        d_context,
        flops=8 * rows * width * columns,
    )
    keep, give = call(
        functools.partial(kv_grads_kernel, sides),
        [shape_of((chips, pad_rows, 2 * columns))] * 2,
        at,
        enc,
        dk,
        dv,
        scratch=[pltpu.VMEM((width, columns), F32)],
        flops=4 * rows * width * columns,
        smem=1,
    )
    grad_kv = scatter_two_axes(keep, give, sides, owners)
    d_encoded = scatter_ring(parts, ranks)
    keep, give = call(
        grads_kernel,
        [shape_of((chips, pad_rows, 2 * hidden))] * 2,
        at,
        *gather_ring(d_encoded, ranks),
        normed,
        act,
        slope,
        out_weight,
        scratch=[pltpu.VMEM((width, hidden), F32)],
        flops=6 * rows * width * hidden,
        smem=1,
    )
    pair = (keep.astype(F32) + swap_cores(give, owners).astype(F32)).astype(BF)
    grads = scatter_chips(pair, owners)
    return (
        context,
        d_queries,
        grad_kv[:out_rows].reshape(out_rows, 2, columns),
        grads[:out_rows, hidden:],
        grads[:out_rows, :hidden].T,
    )


def solution(mesh):
    placed = (
        P("dp", "mp"),
        P(None, "dp", None),
        P("dp"),
        P("dp"),
        P(None, "mp"),
        P("mp", None),
        P(None, None, "mp"),
        P("dp", "mp"),
    )
    return jax.shard_map(
        per_device,
        mesh=mesh,
        in_specs=placed,
        out_specs=(P("dp", "mp"), P("dp", "mp"), P("dp", None, "mp"), P("dp", "mp"), P("mp", "dp")),
        check_vma=False,
    )
```

```python
import functools

import jax
import jax.numpy as jnp
from jax import lax
from jax.experimental import pallas as pl
from jax.experimental.pallas import tpu as pltpu
from jax.sharding import PartitionSpec as P

DH = 128
SPAN = 64
NEIGH = 2
PLACE = 128
OFFSETS = (0, 1, 3, -1, -3, 2, -2, 4)
VMEM_LIMIT = 24 * 1024 * 1024

GELU_C = 0.7978845608028654
GELU_A = 0.044715
EPSILON = 1e-06

BF = jnp.bfloat16
F32 = jnp.float32


def dot_nn(a, b):
    return lax.dot_general(a, b, (((1,), (0,)), ((), ())), preferred_element_type=F32)


def dot_nt(a, b):
    return lax.dot_general(a, b, (((1,), (1,)), ((), ())), preferred_element_type=F32)


def dot_tn(a, b):
    return lax.dot_general(a, b, (((0,), (0,)), ((), ())), preferred_element_type=F32)


def call(kernel, outs, *args, scratch=(), flops=0, after=0):
    moved = sum(a.size * a.dtype.itemsize for a in args)
    moved += sum(o.size * o.dtype.itemsize for o in outs)
    whole = pl.BlockSpec(memory_space=pltpu.VMEM)
    unread = pl.BlockSpec(memory_space=pl.ANY)
    return pl.pallas_call(
        kernel,
        out_shape=outs,
        in_specs=[whole] * (len(args) - after) + [unread] * after,
        out_specs=[whole] * len(outs),
        scratch_shapes=list(scratch),
        compiler_params=pltpu.CompilerParams(vmem_limit_bytes=VMEM_LIMIT),
        cost_estimate=pl.CostEstimate(flops=flops, bytes_accessed=moved, transcendentals=0),
    )(*args)


def shape_of(shape, dtype=BF):
    return jax.ShapeDtypeStruct(shape, dtype)


def place_kernel(tokens, blocks, got_ref, raw_ref):
    rows, width = got_ref.shape
    wide = width - PLACE
    marks = got_ref[:, wide:]
    spread_rows = lax.broadcasted_iota(jnp.int32, (PLACE, blocks * tokens), 0)
    spread_cols = lax.broadcasted_iota(jnp.int32, (PLACE, blocks * tokens), 1)
    spread = (spread_rows == spread_cols // tokens).astype(BF)
    chosen = dot_nn(marks, spread)
    row_token = lax.broadcasted_iota(jnp.int32, chosen.shape, 0) % tokens
    col_token = lax.broadcasted_iota(jnp.int32, chosen.shape, 1) % tokens
    chosen = jnp.where(row_token == col_token, chosen, 0.0).astype(BF)
    raw_ref[...] = dot_tn(chosen, got_ref[:, :wide]).astype(BF)


def join(refs):
    own, p1, p3, m1, m3, p2, m2, low, high = refs
    return jnp.concatenate([r[...] for r in (own, p1, p3, m1, m3, p2, m2, low, high)], axis=0)


def part_shapes(piece, width):
    rows = (piece, 2 * piece, 2 * piece, piece, piece, piece // 2, piece // 2)
    return [shape_of((r, width)) for r in rows]


def write_parts(part, refs):
    at = 0
    for ref in refs:
        rows = ref.shape[0]
        ref[...] = part[at : at + rows]
        at += rows


def relay_kernel(ahead_ref, behind_ref, low_ref, high_ref, p2_ref, m2_ref, p2_out, m2_out):
    piece = p2_ref.shape[0]
    half = piece // 2
    plus = p2_ref[...].astype(F32) + ahead_ref[piece:].astype(F32)
    minus = m2_ref[...].astype(F32) + behind_ref[piece:].astype(F32)
    p2_out[:half] = (plus[:half] + low_ref[...].astype(F32)).astype(BF)
    p2_out[half:] = plus[half:].astype(BF)
    m2_out[:half] = minus[:half].astype(BF)
    m2_out[half:] = (minus[half:] + high_ref[...].astype(F32)).astype(BF)


def sum_kernel(*refs):
    own_ref, ahead_ref, behind_ref, p2_ref, m2_ref = refs[:5]
    piece = own_ref.shape[0]
    total = own_ref[...].astype(F32) + ahead_ref[:piece].astype(F32) + behind_ref[:piece].astype(F32)
    total = total + p2_ref[...].astype(F32) + m2_ref[...].astype(F32)
    for extra in refs[5:-1]:
        total = total + extra[...].astype(F32)
    refs[-1][...] = total.astype(BF)


def shift(array, hops, ranks):
    return lax.ppermute(array, "mp", [(i, (i + hops) % ranks) for i in range(ranks)])


def gather_ring(piece, ranks):
    half = piece.shape[0] // 2
    p1, m1 = shift(piece, -1, ranks), shift(piece, 1, ranks)
    p2, m2 = shift(piece, -2, ranks), shift(piece, 2, ranks)
    p3, m3 = shift(p2, -1, ranks), shift(m2, 1, ranks)
    low, high = shift(p2[:half], -2, ranks), shift(m2[half:], 2, ranks)
    return (piece, p1, p3, m1, m3, p2, m2, low, high)


def scatter_ring(parts, ranks, *extra):
    own, ahead, behind, p2, m2, low, high = parts
    ahead, behind = shift(ahead, 1, ranks), shift(behind, -1, ranks)
    low, high = shift(low, 2, ranks), shift(high, -2, ranks)
    p2, m2 = call(
        relay_kernel,
        [shape_of(p2.shape)] * 2,
        ahead,
        behind,
        low,
        high,
        p2,
        m2,
    )
    p2, m2 = shift(p2, 2, ranks), shift(m2, -2, ranks)
    (total,) = call(sum_kernel, [shape_of(own.shape)], own, ahead, behind, p2, m2, *extra)
    return total


def encode_kernel(*refs):
    win_ref, wout_ref, normed_ref, act_ref, slope_ref = refs[9:14]
    wide = join(refs[:9]).astype(F32)
    mean_square = jnp.mean(wide * wide, axis=-1, keepdims=True)
    normed = (wide * lax.rsqrt(mean_square + EPSILON)).astype(BF)
    normed_ref[...] = normed
    pre = dot_nt(normed, win_ref[...])
    square = pre * pre
    tanh_value = jnp.tanh(GELU_C * (pre + GELU_A * square * pre))
    act = (0.5 * pre * (1.0 + tanh_value)).astype(BF)
    act_ref[...] = act
    slope = 0.5 * (1.0 + tanh_value) + 0.5 * pre * (1.0 - tanh_value * tanh_value) * GELU_C * (
        1.0 + 3.0 * GELU_A * square
    )
    slope_ref[...] = slope.astype(BF)
    write_parts(dot_nn(act, wout_ref[...]).astype(BF), refs[14:])


def deal(core, total_ref, keep_ref, give_ref, cols, slot_of):
    chips = keep_ref.shape[0]
    rows = total_ref.shape[0] // (2 * chips)
    filler = jnp.zeros((keep_ref.shape[1] - rows, total_ref.shape[1]), BF)

    def write(first, second):
        for chip in range(chips):
            at = 2 * chip * rows
            slot = slot_of(chip)
            first[slot, :rows, cols] = total_ref[at : at + rows, :].astype(BF)
            second[slot, :rows, cols] = total_ref[at + rows : at + 2 * rows, :].astype(BF)
            if filler.shape[0]:
                first[slot, rows:, cols] = filler
                second[slot, rows:, cols] = filler

    @pl.when(core == 0)
    def _():
        write(keep_ref, give_ref)

    @pl.when(core != 0)
    def _():
        write(give_ref, keep_ref)


def attend_kernel(spans, ranks, *refs):
    kw_ref, vw_ref, q_ref, g_ref, ctx_ref, dq_ref, enc_ref, dk_ref, dv_ref = refs[9:18]
    scaling = DH ** (-0.5)
    enc = join(refs[:9])
    enc_ref[...] = enc
    rows, columns = dk_ref.shape
    piece = rows // ranks // spans
    cut = (ranks, spans, piece, columns)
    keys = dot_nn(enc, kw_ref[...]).astype(BF).reshape(cut)
    values = dot_nn(enc, vw_ref[...]).astype(BF).reshape(cut)
    for s in range(spans):
        q_rows = slice(s * SPAN, (s + 1) * SPAN)
        for h in range(columns // DH):
            cols = slice(h * DH, (h + 1) * DH)
            k = keys[:, s, :, cols].reshape(ranks * piece, DH)
            v = values[:, s, :, cols].reshape(ranks * piece, DH)
            q = q_ref[q_rows, cols]
            g = g_ref[q_rows, cols]
            scores = dot_nt(q, k) * scaling
            peak = jnp.max(scores, axis=-1, keepdims=True)
            weights = jnp.exp(scores - peak)
            probs_wide = weights / jnp.sum(weights, axis=-1, keepdims=True)
            probs = probs_wide.astype(BF)
            ctx_ref[q_rows, cols] = dot_nn(probs, v).astype(BF)
            d_probs = dot_nt(g, v)
            inner = jnp.sum(d_probs * probs_wide, axis=-1, keepdims=True)
            d_scores = (probs_wide * (d_probs - inner) * scaling).astype(BF)
            dq_ref[q_rows, cols] = dot_nn(d_scores, k).astype(BF)
            d_k = dot_tn(d_scores, q).astype(BF)
            d_v = dot_tn(probs, g).astype(BF)
            for r in range(ranks):
                at = (r * spans + s) * piece
                dk_ref[at : at + piece, cols] = d_k[r * piece : (r + 1) * piece]
                dv_ref[at : at + piece, cols] = d_v[r * piece : (r + 1) * piece]
    part = (dot_nt(dk_ref[...], kw_ref[...]) + dot_nt(dv_ref[...], vw_ref[...])).astype(BF)
    write_parts(part, refs[18:])


def kv_grads_kernel(sides, enc_ref, dk_ref, dv_ref, keep_ref, give_ref, total_ref):
    columns = dk_ref.shape[1]
    me = lax.axis_index("dp")
    core, my_x, my_y = me % 2, me // 2 // sides[1], me // 2 % sides[1]

    def slot_of(chip):
        x, y = chip // sides[1], chip % sides[1]
        ahead = (x - my_x + sides[0]) % sides[0]
        beside = (y - my_y + sides[1]) % sides[1]
        return ahead * sides[1] + beside

    enc = enc_ref[...]
    total_ref[...] = dot_tn(enc, dk_ref[...])
    deal(core, total_ref, keep_ref, give_ref, slice(0, columns), slot_of)
    total_ref[...] = dot_tn(enc, dv_ref[...])
    deal(core, total_ref, keep_ref, give_ref, slice(columns, 2 * columns), slot_of)


def grads_kernel(*refs):
    normed_ref, act_ref, slope_ref, wout_ref, _, keep_ref, give_ref, total_ref = refs[9:]
    hidden = act_ref.shape[1]
    core = lax.axis_index("dp") % 2
    d_enc = join(refs[:9])
    total_ref[...] = dot_tn(d_enc, act_ref[...])
    deal(core, total_ref, keep_ref, give_ref, slice(0, hidden), lambda chip: chip)
    d_pre = (dot_nt(d_enc, wout_ref[...]) * slope_ref[...].astype(F32)).astype(BF)
    total_ref[...] = dot_tn(normed_ref[...], d_pre)
    deal(core, total_ref, keep_ref, give_ref, slice(hidden, 2 * hidden), lambda chip: chip)


def swap_cores(give, devices):
    return lax.ppermute(give, "dp", [(i, i ^ 1) for i in range(devices)])


def scatter_chips(pair, devices):
    chips = devices // 2
    groups = [[chip * 2 + c for chip in range(chips)] for c in range(2)]
    every = lax.all_to_all(pair, "dp", 0, 0, axis_index_groups=groups, tiled=True)
    return jnp.sum(every.astype(F32), axis=0)


def scatter_axis(pieces, size, stride, devices):
    total = pieces[0].astype(F32)
    for k in range(1, size):
        perm = []
        for i in range(devices):
            at = i // stride % size
            perm.append((i, i + ((at + k) % size - at) * stride))
        total = total + lax.ppermute(pieces[k], "dp", perm).astype(F32)
    return total


def scatter_across(keep, give, sides, devices):
    got = swap_cores(give, devices)
    across, beside = sides
    cut = (across, beside) + keep.shape[1:]
    keep, got = keep.reshape(cut), got.reshape(cut)
    pieces = [(keep[k].astype(F32) + got[k].astype(F32)).astype(BF) for k in range(across)]
    return scatter_axis(pieces, across, 2 * beside, devices).astype(BF)


def per_device(queries, neighbours, targets, counts, in_weight, out_weight, kv_weight, d_context):
    length, holding, width = neighbours.shape
    owners = lax.axis_size("dp")
    ranks = lax.axis_size("mp")
    tokens = length // ranks
    token_rows, columns = queries.shape
    hidden = in_weight.shape[1]
    spans = token_rows // SPAN
    blocks = NEIGH * spans
    my_rank = lax.axis_index("mp")
    across = 1
    while across * across < owners // 2:
        across *= 2
    sides = (across, owners // 2 // across)
    piece = blocks * tokens
    rows = ranks * piece
    chips = owners // 2
    out_rows = width // owners
    pad_rows = -(-out_rows // 16) * 16

    own = lax.dynamic_slice_in_dim(neighbours, my_rank * tokens, tokens, 0).reshape(tokens * holding, width)
    is_live = jnp.arange(holding, dtype=jnp.int32) < counts[0]
    dest = jnp.where(is_live, targets // blocks, -1)
    place = targets % blocks
    marks = jnp.arange(PLACE, dtype=jnp.int32)[None, :] == jnp.tile(place, tokens)[:, None]
    payload = jnp.concatenate([own, marks.astype(BF)], axis=1)
    row_ids = jnp.arange(owners * tokens, dtype=jnp.int32)
    col_ids = jnp.arange(tokens * holding, dtype=jnp.int32)
    pick = jnp.logical_and(
        (row_ids // tokens)[:, None] == jnp.tile(dest, tokens)[None, :],
        (row_ids % tokens)[:, None] == (col_ids // holding)[None, :],
    ).astype(BF)
    sent = dot_nn(pick, payload).astype(BF).reshape(owners, tokens, width + PLACE)
    got = lax.all_to_all(sent, "dp", 0, 0, tiled=True).reshape(owners * tokens, width + PLACE)
    (raw,) = call(
        functools.partial(place_kernel, tokens, blocks),
        [shape_of((piece, width))],
        got,
        flops=2 * owners * tokens * piece * width,
    )
    normed, act, slope, *parts = call(
        encode_kernel,
        [
            shape_of((rows, width)),
            shape_of((rows, hidden)),
            shape_of((rows, hidden)),
            *part_shapes(piece, width),
        ],
        *gather_ring(raw, ranks),
        in_weight.T,
        out_weight,
        flops=4 * rows * width * hidden,
    )
    encoded = scatter_ring(parts, ranks, raw)
    context, d_queries, enc, dk, dv, *parts = call(
        functools.partial(attend_kernel, spans, ranks),
        [
            shape_of((token_rows, columns)),
            shape_of((token_rows, columns)),
            shape_of((rows, width)),
            shape_of((rows, columns)),
            shape_of((rows, columns)),
            *part_shapes(piece, width),
        ],
        *gather_ring(encoded, ranks),
        kv_weight[:, 0, :],
        kv_weight[:, 1, :],
        queries,
        d_context,
        flops=8 * rows * width * columns,
    )
    keep, give = call(
        functools.partial(kv_grads_kernel, sides),
        [shape_of((chips, pad_rows, 2 * columns))] * 2,
        enc,
        dk,
        dv,
        scratch=[pltpu.VMEM((width, columns), F32)],
        flops=4 * rows * width * columns,
    )
    half_kv = scatter_across(keep, give, sides, owners)
    d_encoded = scatter_ring(parts, ranks)
    keep, give = call(
        grads_kernel,
        [shape_of((chips, pad_rows, 2 * hidden))] * 2,
        *gather_ring(d_encoded, ranks),
        normed,
        act,
        slope,
        out_weight,
        half_kv,
        scratch=[pltpu.VMEM((width, hidden), F32)],
        flops=6 * rows * width * hidden,
        after=1,
    )
    grad_kv = scatter_axis([half_kv[k] for k in range(sides[1])], sides[1], 2, owners)
    pair = (keep.astype(F32) + swap_cores(give, owners).astype(F32)).astype(BF)
    grads = scatter_chips(pair, owners)
    return (
        context,
        d_queries,
        grad_kv[:out_rows].reshape(out_rows, 2, columns),
        grads[:out_rows, hidden:],
        grads[:out_rows, :hidden].T,
    )


def solution(mesh):
    placed = (
        P("dp", "mp"),
        P(None, "dp", None),
        P("dp"),
        P("dp"),
        P(None, "mp"),
        P("mp", None),
        P(None, None, "mp"),
        P("dp", "mp"),
    )
    return jax.shard_map(
        per_device,
        mesh=mesh,
        in_specs=placed,
        out_specs=(P("dp", "mp"), P("dp", "mp"), P("dp", None, "mp"), P("dp", "mp"), P("mp", "dp")),
        check_vma=False,
    )
```

```python
import functools

import jax
import jax.numpy as jnp
from jax import lax
from jax.experimental import pallas as pl
from jax.experimental.pallas import tpu as pltpu
from jax.sharding import PartitionSpec as P

DH = 128
SPAN = 64
NEIGH = 2
PLACE = 128
OFFSETS = (0, 1, 3, -1, -3, 2, -2, 4)
VMEM_LIMIT = 24 * 1024 * 1024

GELU_C = 0.7978845608028654
GELU_A = 0.044715
EPSILON = 1e-06

BF = jnp.bfloat16
F32 = jnp.float32


def dot_nn(a, b):
    return lax.dot_general(a, b, (((1,), (0,)), ((), ())), preferred_element_type=F32)


def dot_nt(a, b):
    return lax.dot_general(a, b, (((1,), (1,)), ((), ())), preferred_element_type=F32)


def dot_tn(a, b):
    return lax.dot_general(a, b, (((0,), (0,)), ((), ())), preferred_element_type=F32)


def call(kernel, outs, *args, scratch=(), flops=0, after=0):
    moved = sum(a.size * a.dtype.itemsize for a in args)
    moved += sum(o.size * o.dtype.itemsize for o in outs)
    whole = pl.BlockSpec(memory_space=pltpu.VMEM)
    unread = pl.BlockSpec(memory_space=pl.ANY)
    return pl.pallas_call(
        kernel,
        out_shape=outs,
        in_specs=[whole] * (len(args) - after) + [unread] * after,
        out_specs=[whole] * len(outs),
        scratch_shapes=list(scratch),
        compiler_params=pltpu.CompilerParams(vmem_limit_bytes=VMEM_LIMIT),
        cost_estimate=pl.CostEstimate(flops=flops, bytes_accessed=moved, transcendentals=0),
    )(*args)


def shape_of(shape, dtype=BF):
    return jax.ShapeDtypeStruct(shape, dtype)


def place_kernel(tokens, blocks, got_ref, raw_ref):
    rows, width = got_ref.shape
    wide = width - PLACE
    marks = got_ref[:, wide:]
    spread_rows = lax.broadcasted_iota(jnp.int32, (PLACE, blocks * tokens), 0)
    spread_cols = lax.broadcasted_iota(jnp.int32, (PLACE, blocks * tokens), 1)
    spread = (spread_rows == spread_cols // tokens).astype(BF)
    chosen = dot_nn(marks, spread)
    row_token = lax.broadcasted_iota(jnp.int32, chosen.shape, 0) % tokens
    col_token = lax.broadcasted_iota(jnp.int32, chosen.shape, 1) % tokens
    chosen = jnp.where(row_token == col_token, chosen, 0.0).astype(BF)
    raw_ref[...] = dot_tn(chosen, got_ref[:, :wide]).astype(BF)


def join(refs):
    return jnp.concatenate([r[...] for r in refs], axis=0)


def part_shapes(piece, width):
    return [shape_of((r * piece, width)) for r in (1, 2, 2, 1, 1, 1)]


def write_parts(part, refs):
    at = 0
    for ref in refs:
        rows = ref.shape[0]
        ref[...] = part[at : at + rows]
        at += rows


def on_first_core():
    return jnp.full((1, 1), lax.axis_index("dp") % 2) == 0


def pick_kernel(first_ref, second_ref, out_ref):
    out_ref[...] = jnp.where(on_first_core(), first_ref[...], second_ref[...])


def relay_kernel(ahead_ref, behind_ref, far_ref, p2_ref, m2_ref, p2_out, m2_out):
    piece = p2_ref.shape[0]
    far = far_ref[...].astype(F32)
    first = on_first_core()
    plus = p2_ref[...].astype(F32) + ahead_ref[piece:].astype(F32)
    minus = m2_ref[...].astype(F32) + behind_ref[piece:].astype(F32)
    p2_out[...] = (plus + jnp.where(first, far, 0.0)).astype(BF)
    m2_out[...] = (minus + jnp.where(first, 0.0, far)).astype(BF)


def sum_kernel(*refs):
    own_ref, ahead_ref, behind_ref, p2_ref, m2_ref = refs[:5]
    piece = own_ref.shape[0]
    total = own_ref[...].astype(F32) + ahead_ref[:piece].astype(F32) + behind_ref[:piece].astype(F32)
    total = total + p2_ref[...].astype(F32) + m2_ref[...].astype(F32)
    for extra in refs[5:-1]:
        total = total + extra[...].astype(F32)
    refs[-1][...] = total.astype(BF)


def shift(array, hops, ranks):
    return lax.ppermute(array, "mp", [(i, (i + hops) % ranks) for i in range(ranks)])


def shift_by_core(array, hops, ranks):
    perm = []
    for i in range(lax.axis_size("dp")):
        step = hops if i % 2 == 0 else -hops
        perm += [(i * ranks + j, i * ranks + (j + step) % ranks) for j in range(ranks)]
    return lax.ppermute(array, ("dp", "mp"), perm)


def gather_ring(piece, ranks):
    p2, m2 = shift(piece, -2, ranks), shift(piece, 2, ranks)
    p1, m1 = shift(piece, -1, ranks), shift(piece, 1, ranks)
    (far,) = call(pick_kernel, [shape_of(piece.shape)], p2, m2)
    far = shift_by_core(far, -2, ranks)
    p3, m3 = shift(p2, -1, ranks), shift(m2, 1, ranks)
    return (piece, p1, p3, m1, m3, p2, m2, far)


def scatter_ring(parts, ranks, *extra, beside=None):
    own, ahead, behind, p2, m2, far = parts
    far = shift_by_core(far, 2, ranks)
    ahead, behind = shift(ahead, 1, ranks), shift(behind, -1, ranks)
    p2, m2 = call(relay_kernel, [shape_of(p2.shape)] * 2, ahead, behind, far, p2, m2)
    kept = beside(p2) if beside else None
    p2, m2 = shift(p2, 2, ranks), shift(m2, -2, ranks)
    (total,) = call(sum_kernel, [shape_of(own.shape)], own, ahead, behind, p2, m2, *extra)
    return total, kept


def encode_kernel(*refs):
    win_ref, wout_ref, normed_ref, act_ref, slope_ref = refs[8:13]
    wide = join(refs[:8]).astype(F32)
    mean_square = jnp.mean(wide * wide, axis=-1, keepdims=True)
    normed = (wide * lax.rsqrt(mean_square + EPSILON)).astype(BF)
    normed_ref[...] = normed
    pre = dot_nt(normed, win_ref[...])
    square = pre * pre
    tanh_value = jnp.tanh(GELU_C * (pre + GELU_A * square * pre))
    act = (0.5 * pre * (1.0 + tanh_value)).astype(BF)
    act_ref[...] = act
    slope = 0.5 * (1.0 + tanh_value) + 0.5 * pre * (1.0 - tanh_value * tanh_value) * GELU_C * (
        1.0 + 3.0 * GELU_A * square
    )
    slope_ref[...] = slope.astype(BF)
    write_parts(dot_nn(act, wout_ref[...]).astype(BF), refs[13:])


def deal(core, total_ref, keep_ref, give_ref, cols, slot_of):
    chips = keep_ref.shape[0]
    rows = total_ref.shape[0] // (2 * chips)
    filler = jnp.zeros((keep_ref.shape[1] - rows, total_ref.shape[1]), BF)

    def write(first, second):
        for chip in range(chips):
            at = 2 * chip * rows
            slot = slot_of(chip)
            first[slot, :rows, cols] = total_ref[at : at + rows, :].astype(BF)
            second[slot, :rows, cols] = total_ref[at + rows : at + 2 * rows, :].astype(BF)
            if filler.shape[0]:
                first[slot, rows:, cols] = filler
                second[slot, rows:, cols] = filler

    @pl.when(core == 0)
    def _():
        write(keep_ref, give_ref)

    @pl.when(core != 0)
    def _():
        write(give_ref, keep_ref)


def attend_kernel(spans, ranks, *refs):
    kw_ref, vw_ref, q_ref, g_ref, ctx_ref, dq_ref, enc_ref, dk_ref, dv_ref = refs[8:17]
    scaling = DH ** (-0.5)
    enc = join(refs[:8])
    enc_ref[...] = enc
    rows, columns = dk_ref.shape
    piece = rows // ranks // spans
    cut = (ranks, spans, piece, columns)
    keys = dot_nn(enc, kw_ref[...]).astype(BF).reshape(cut)
    values = dot_nn(enc, vw_ref[...]).astype(BF).reshape(cut)
    for s in range(spans):
        q_rows = slice(s * SPAN, (s + 1) * SPAN)
        heads = [slice(h * DH, (h + 1) * DH) for h in range(columns // DH)]
        ks = [keys[:, s, :, cols].reshape(ranks * piece, DH) for cols in heads]
        vs = [values[:, s, :, cols].reshape(ranks * piece, DH) for cols in heads]
        qs = [q_ref[q_rows, cols] for cols in heads]
        gs = [g_ref[q_rows, cols] for cols in heads]
        scores = [dot_nt(q, k) * scaling for q, k in zip(qs, ks)]
        d_probs = [dot_nt(g, v) for g, v in zip(gs, vs)]
        wide = []
        for x in scores:
            weights = jnp.exp(x - jnp.max(x, axis=-1, keepdims=True))
            wide.append(weights / jnp.sum(weights, axis=-1, keepdims=True))
        probs = [x.astype(BF) for x in wide]
        d_scores = [
            (p * (d - jnp.sum(d * p, axis=-1, keepdims=True)) * scaling).astype(BF)
            for p, d in zip(wide, d_probs)
        ]
        for cols, p, d, k, v, q, g in zip(heads, probs, d_scores, ks, vs, qs, gs):
            ctx_ref[q_rows, cols] = dot_nn(p, v).astype(BF)
            dq_ref[q_rows, cols] = dot_nn(d, k).astype(BF)
            d_k = dot_tn(d, q).astype(BF)
            d_v = dot_tn(p, g).astype(BF)
            for r in range(ranks):
                at = (r * spans + s) * piece
                dk_ref[at : at + piece, cols] = d_k[r * piece : (r + 1) * piece]
                dv_ref[at : at + piece, cols] = d_v[r * piece : (r + 1) * piece]
    part = (dot_nt(dk_ref[...], kw_ref[...]) + dot_nt(dv_ref[...], vw_ref[...])).astype(BF)
    write_parts(part, refs[17:])


def kv_grads_kernel(sides, enc_ref, dk_ref, dv_ref, _, keep_ref, give_ref, total_ref):
    columns = dk_ref.shape[1]
    me = lax.axis_index("dp")
    core, my_x, my_y = me % 2, me // 2 // sides[1], me // 2 % sides[1]

    def slot_of(chip):
        x, y = chip // sides[1], chip % sides[1]
        ahead = (x - my_x + sides[0]) % sides[0]
        beside = (y - my_y + sides[1]) % sides[1]
        return ahead * sides[1] + beside

    enc = enc_ref[...]
    total_ref[...] = dot_tn(enc, dk_ref[...])
    deal(core, total_ref, keep_ref, give_ref, slice(0, columns), slot_of)
    total_ref[...] = dot_tn(enc, dv_ref[...])
    deal(core, total_ref, keep_ref, give_ref, slice(columns, 2 * columns), slot_of)


def grads_kernel(*refs):
    normed_ref, act_ref, slope_ref, wout_ref, keep_ref, give_ref, total_ref = refs[8:]
    hidden = act_ref.shape[1]
    core = lax.axis_index("dp") % 2
    d_enc = join(refs[:8])
    total_ref[...] = dot_tn(d_enc, act_ref[...])
    deal(core, total_ref, keep_ref, give_ref, slice(0, hidden), lambda chip: chip)
    d_pre = (dot_nt(d_enc, wout_ref[...]) * slope_ref[...].astype(F32)).astype(BF)
    total_ref[...] = dot_tn(normed_ref[...], d_pre)
    deal(core, total_ref, keep_ref, give_ref, slice(hidden, 2 * hidden), lambda chip: chip)


def total_kernel(every_ref, first_ref, second_ref):
    total = every_ref[0].astype(F32)
    for chip in range(1, every_ref.shape[0]):
        total = total + every_ref[chip].astype(F32)
    rows, hidden = first_ref.shape
    first_ref[...] = total[:rows, :hidden]
    second_ref[...] = total[:rows, hidden:]


def swap_cores(give, devices):
    return lax.ppermute(give, "dp", [(i, i ^ 1) for i in range(devices)])


def scatter_chips(pair, devices):
    chips = devices // 2
    groups = [[chip * 2 + c for chip in range(chips)] for c in range(2)]
    return lax.all_to_all(pair, "dp", 0, 0, axis_index_groups=groups, tiled=True)


def scatter_axis(pieces, size, stride, devices):
    total = pieces[0].astype(F32)
    for k in range(1, size):
        perm = []
        for i in range(devices):
            at = i // stride % size
            perm.append((i, i + ((at + k) % size - at) * stride))
        total = total + lax.ppermute(pieces[k], "dp", perm).astype(F32)
    return total


def scatter_across(keep, give, sides, devices):
    got = swap_cores(give, devices)
    across, beside = sides
    cut = (across, beside) + keep.shape[1:]
    keep, got = keep.reshape(cut), got.reshape(cut)
    pieces = [(keep[k].astype(F32) + got[k].astype(F32)).astype(BF) for k in range(across)]
    return scatter_axis(pieces, across, 2 * beside, devices).astype(BF)


def per_device(queries, neighbours, targets, counts, in_weight, out_weight, kv_weight, d_context):
    length, holding, width = neighbours.shape
    owners = lax.axis_size("dp")
    ranks = lax.axis_size("mp")
    tokens = length // ranks
    token_rows, columns = queries.shape
    hidden = in_weight.shape[1]
    spans = token_rows // SPAN
    blocks = NEIGH * spans
    my_rank = lax.axis_index("mp")
    across = 1
    while across * across < owners // 2:
        across *= 2
    sides = (across, owners // 2 // across)
    piece = blocks * tokens
    rows = ranks * piece
    chips = owners // 2
    out_rows = width // owners
    pad_rows = -(-out_rows // 16) * 16

    own = lax.dynamic_slice_in_dim(neighbours, my_rank * tokens, tokens, 0).reshape(tokens * holding, width)
    is_live = jnp.arange(holding, dtype=jnp.int32) < counts[0]
    dest = jnp.where(is_live, targets // blocks, -1)
    place = targets % blocks
    marks = jnp.arange(PLACE, dtype=jnp.int32)[None, :] == jnp.tile(place, tokens)[:, None]
    payload = jnp.concatenate([own, marks.astype(BF)], axis=1)
    row_ids = jnp.arange(owners * tokens, dtype=jnp.int32)
    col_ids = jnp.arange(tokens * holding, dtype=jnp.int32)
    pick = jnp.logical_and(
        (row_ids // tokens)[:, None] == jnp.tile(dest, tokens)[None, :],
        (row_ids % tokens)[:, None] == (col_ids // holding)[None, :],
    ).astype(BF)
    sent = dot_nn(pick, payload).astype(BF).reshape(owners, tokens, width + PLACE)
    got = lax.all_to_all(sent, "dp", 0, 0, tiled=True).reshape(owners * tokens, width + PLACE)
    (raw,) = call(
        functools.partial(place_kernel, tokens, blocks),
        [shape_of((piece, width))],
        got,
        flops=2 * owners * tokens * piece * width,
    )
    normed, act, slope, *parts = call(
        encode_kernel,
        [
            shape_of((rows, width)),
            shape_of((rows, hidden)),
            shape_of((rows, hidden)),
            *part_shapes(piece, width),
        ],
        *gather_ring(raw, ranks),
        in_weight.T,
        out_weight,
        flops=4 * rows * width * hidden,
    )
    encoded, _ = scatter_ring(parts, ranks, raw)
    context, d_queries, enc, dk, dv, *parts = call(
        functools.partial(attend_kernel, spans, ranks),
        [
            shape_of((token_rows, columns)),
            shape_of((token_rows, columns)),
            shape_of((rows, width)),
            shape_of((rows, columns)),
            shape_of((rows, columns)),
            *part_shapes(piece, width),
        ],
        *gather_ring(encoded, ranks),
        kv_weight[:, 0, :],
        kv_weight[:, 1, :],
        queries,
        d_context,
        flops=8 * rows * width * columns,
    )

    def kv_grads(relayed):
        keep, give = call(
            functools.partial(kv_grads_kernel, sides),
            [shape_of((chips, pad_rows, 2 * columns))] * 2,
            enc,
            dk,
            dv,
            relayed,
            scratch=[pltpu.VMEM((width, columns), F32)],
            flops=4 * rows * width * columns,
            after=1,
        )
        return scatter_across(keep, give, sides, owners)

    d_encoded, half_kv = scatter_ring(parts, ranks, beside=kv_grads)
    keep, give = call(
        grads_kernel,
        [shape_of((chips, pad_rows, 2 * hidden))] * 2,
        *gather_ring(d_encoded, ranks),
        normed,
        act,
        slope,
        out_weight,
        scratch=[pltpu.VMEM((width, hidden), F32)],
        flops=6 * rows * width * hidden,
    )
    grad_kv = scatter_axis([half_kv[k] for k in range(sides[1])], sides[1], 2, owners)
    pair = (keep.astype(F32) + swap_cores(give, owners).astype(F32)).astype(BF)
    grad_out_t, grad_in = call(
        total_kernel, [shape_of((out_rows, hidden), F32)] * 2, scatter_chips(pair, owners)
    )
    return (
        context,
        d_queries,
        grad_kv[:out_rows].reshape(out_rows, 2, columns),
        grad_in,
        grad_out_t.T,
    )


def solution(mesh):
    placed = (
        P("dp", "mp"),
        P(None, "dp", None),
        P("dp"),
        P("dp"),
        P(None, "mp"),
        P("mp", None),
        P(None, None, "mp"),
        P("dp", "mp"),
    )
    return jax.shard_map(
        per_device,
        mesh=mesh,
        in_specs=placed,
        out_specs=(P("dp", "mp"), P("dp", "mp"), P("dp", None, "mp"), P("dp", "mp"), P("mp", "dp")),
        check_vma=False,
    )
```

```python
import functools

import jax
import jax.numpy as jnp
from jax import lax
from jax.experimental import pallas as pl
from jax.experimental.pallas import tpu as pltpu
from jax.sharding import PartitionSpec as P

DH = 128
SPAN = 64
NEIGH = 2
PLACE = 128
OFFSETS = (0, 1, 3, -1, -3, 2, -2, 4)
VMEM_LIMIT = 24 * 1024 * 1024

GELU_C = 0.7978845608028654
GELU_A = 0.044715
EPSILON = 1e-06

BF = jnp.bfloat16
F32 = jnp.float32


def dot_nn(a, b):
    return lax.dot_general(a, b, (((1,), (0,)), ((), ())), preferred_element_type=F32)


def dot_nt(a, b):
    return lax.dot_general(a, b, (((1,), (1,)), ((), ())), preferred_element_type=F32)


def dot_tn(a, b):
    return lax.dot_general(a, b, (((0,), (0,)), ((), ())), preferred_element_type=F32)


def call(kernel, outs, *args, scratch=(), flops=0, after=0):
    moved = sum(a.size * a.dtype.itemsize for a in args)
    moved += sum(o.size * o.dtype.itemsize for o in outs)
    whole = pl.BlockSpec(memory_space=pltpu.VMEM)
    unread = pl.BlockSpec(memory_space=pl.ANY)
    return pl.pallas_call(
        kernel,
        out_shape=outs,
        in_specs=[whole] * (len(args) - after) + [unread] * after,
        out_specs=[whole] * len(outs),
        scratch_shapes=list(scratch),
        compiler_params=pltpu.CompilerParams(vmem_limit_bytes=VMEM_LIMIT),
        cost_estimate=pl.CostEstimate(flops=flops, bytes_accessed=moved, transcendentals=0),
    )(*args)


def shape_of(shape, dtype=BF):
    return jax.ShapeDtypeStruct(shape, dtype)


def place_kernel(tokens, blocks, got_ref, raw_ref):
    rows, width = got_ref.shape
    wide = width - PLACE
    marks = got_ref[:, wide:]
    spread_rows = lax.broadcasted_iota(jnp.int32, (PLACE, blocks * tokens), 0)
    spread_cols = lax.broadcasted_iota(jnp.int32, (PLACE, blocks * tokens), 1)
    spread = (spread_rows == spread_cols // tokens).astype(BF)
    chosen = dot_nn(marks, spread)
    row_token = lax.broadcasted_iota(jnp.int32, chosen.shape, 0) % tokens
    col_token = lax.broadcasted_iota(jnp.int32, chosen.shape, 1) % tokens
    chosen = jnp.where(row_token == col_token, chosen, 0.0).astype(BF)
    raw_ref[...] = dot_tn(chosen, got_ref[:, :wide]).astype(BF)


def join(refs):
    return jnp.concatenate([r[...] for r in refs], axis=0)


def part_shapes(piece, width):
    return [shape_of((r * piece, width)) for r in (1, 2, 2, 1, 1, 1)]


def write_parts(part, refs):
    at = 0
    for ref in refs:
        rows = ref.shape[0]
        ref[...] = part[at : at + rows]
        at += rows


def on_first_core():
    return jnp.full((1, 1), lax.axis_index("dp") % 2) == 0


def pick_kernel(first_ref, second_ref, out_ref):
    out_ref[...] = jnp.where(on_first_core(), first_ref[...], second_ref[...])


def relay_kernel(ahead_ref, behind_ref, far_ref, p2_ref, m2_ref, p2_out, m2_out):
    piece = p2_ref.shape[0]
    far = far_ref[...].astype(F32)
    first = on_first_core()
    plus = p2_ref[...].astype(F32) + ahead_ref[piece:].astype(F32)
    minus = m2_ref[...].astype(F32) + behind_ref[piece:].astype(F32)
    p2_out[...] = (plus + jnp.where(first, far, 0.0)).astype(BF)
    m2_out[...] = (minus + jnp.where(first, 0.0, far)).astype(BF)


def sum_kernel(*refs):
    own_ref, ahead_ref, behind_ref, p2_ref, m2_ref = refs[:5]
    piece = own_ref.shape[0]
    total = own_ref[...].astype(F32) + ahead_ref[:piece].astype(F32) + behind_ref[:piece].astype(F32)
    total = total + p2_ref[...].astype(F32) + m2_ref[...].astype(F32)
    for extra in refs[5:-1]:
        total = total + extra[...].astype(F32)
    refs[-1][...] = total.astype(BF)


def shift(array, hops, ranks):
    return lax.ppermute(array, "mp", [(i, (i + hops) % ranks) for i in range(ranks)])


def shift_by_core(array, hops, ranks):
    perm = []
    for i in range(lax.axis_size("dp")):
        step = hops if i % 2 == 0 else -hops
        perm += [(i * ranks + j, i * ranks + (j + step) % ranks) for j in range(ranks)]
    return lax.ppermute(array, ("dp", "mp"), perm)


def gather_ring(piece, ranks):
    p2, m2 = shift(piece, -2, ranks), shift(piece, 2, ranks)
    p1, m1 = shift(piece, -1, ranks), shift(piece, 1, ranks)
    (far,) = call(pick_kernel, [shape_of(piece.shape)], p2, m2)
    far = shift_by_core(far, -2, ranks)
    p3, m3 = shift(p2, -1, ranks), shift(m2, 1, ranks)
    return (piece, p1, p3, m1, m3, p2, m2, far)


def scatter_ring(parts, ranks, *extra, beside=None):
    own, ahead, behind, p2, m2, far = parts
    far = shift_by_core(far, 2, ranks)
    ahead, behind = shift(ahead, 1, ranks), shift(behind, -1, ranks)
    p2, m2 = call(relay_kernel, [shape_of(p2.shape)] * 2, ahead, behind, far, p2, m2)
    kept = beside(p2) if beside else None
    p2, m2 = shift(p2, 2, ranks), shift(m2, -2, ranks)
    (total,) = call(sum_kernel, [shape_of(own.shape)], own, ahead, behind, p2, m2, *extra)
    return total, kept


def encode_kernel(*refs):
    win_ref, wout_ref, normed_ref, act_ref, slope_ref = refs[8:13]
    wide = join(refs[:8]).astype(F32)
    mean_square = jnp.mean(wide * wide, axis=-1, keepdims=True)
    normed = (wide * lax.rsqrt(mean_square + EPSILON)).astype(BF)
    normed_ref[...] = normed
    pre = dot_nt(normed, win_ref[...])
    square = pre * pre
    tanh_value = jnp.tanh(GELU_C * (pre + GELU_A * square * pre))
    act = (0.5 * pre * (1.0 + tanh_value)).astype(BF)
    act_ref[...] = act
    slope = 0.5 * (1.0 + tanh_value) + 0.5 * pre * (1.0 - tanh_value * tanh_value) * GELU_C * (
        1.0 + 3.0 * GELU_A * square
    )
    slope_ref[...] = slope.astype(BF)
    write_parts(dot_nn(act, wout_ref[...]).astype(BF), refs[13:])


def deal(core, total_ref, keep_ref, give_ref, cols, slots=None):
    chips = keep_ref.shape[0]
    rows = total_ref.shape[0] // (2 * chips)
    filler = jnp.zeros((keep_ref.shape[1] - rows, total_ref.shape[1]), BF)

    def write(refs):
        for chip in range(chips):
            for kind, ref in enumerate(refs):
                at = (2 * chip + kind) * rows
                slot = slots(chip)[kind] if slots else chip
                ref[slot, :rows, cols] = total_ref[at : at + rows, :].astype(BF)
                if filler.shape[0]:
                    ref[slot, rows:, cols] = filler

    @pl.when(core == 0)
    def _():
        write((keep_ref, give_ref))

    @pl.when(core != 0)
    def _():
        write((give_ref, keep_ref))


def attend_kernel(spans, ranks, *refs):
    kw_ref, vw_ref, q_ref, g_ref, ctx_ref, dq_ref, enc_ref, dk_ref, dv_ref = refs[8:17]
    scaling = DH ** (-0.5)
    enc = join(refs[:8])
    enc_ref[...] = enc
    rows, columns = dk_ref.shape
    piece = rows // ranks // spans
    cut = (ranks, spans, piece, columns)
    keys = dot_nn(enc, kw_ref[...]).astype(BF).reshape(cut)
    values = dot_nn(enc, vw_ref[...]).astype(BF).reshape(cut)
    for s in range(spans):
        q_rows = slice(s * SPAN, (s + 1) * SPAN)
        heads = [slice(h * DH, (h + 1) * DH) for h in range(columns // DH)]
        ks = [keys[:, s, :, cols].reshape(ranks * piece, DH) for cols in heads]
        vs = [values[:, s, :, cols].reshape(ranks * piece, DH) for cols in heads]
        qs = [q_ref[q_rows, cols] for cols in heads]
        gs = [g_ref[q_rows, cols] for cols in heads]
        scores = [dot_nt(q, k) * scaling for q, k in zip(qs, ks)]
        d_probs = [dot_nt(g, v) for g, v in zip(gs, vs)]
        wide = []
        for x in scores:
            weights = jnp.exp(x - jnp.max(x, axis=-1, keepdims=True))
            wide.append(weights / jnp.sum(weights, axis=-1, keepdims=True))
        probs = [x.astype(BF) for x in wide]
        d_scores = [
            (p * (d - jnp.sum(d * p, axis=-1, keepdims=True)) * scaling).astype(BF)
            for p, d in zip(wide, d_probs)
        ]
        for cols, p, d, k, v, q, g in zip(heads, probs, d_scores, ks, vs, qs, gs):
            ctx_ref[q_rows, cols] = dot_nn(p, v).astype(BF)
            dq_ref[q_rows, cols] = dot_nn(d, k).astype(BF)
            d_k = dot_tn(d, q).astype(BF)
            d_v = dot_tn(p, g).astype(BF)
            for r in range(ranks):
                at = (r * spans + s) * piece
                dk_ref[at : at + piece, cols] = d_k[r * piece : (r + 1) * piece]
                dv_ref[at : at + piece, cols] = d_v[r * piece : (r + 1) * piece]
    part = (dot_nt(dk_ref[...], kw_ref[...]) + dot_nt(dv_ref[...], vw_ref[...])).astype(BF)
    write_parts(part, refs[17:])


def kv_grads_kernel(sides, enc_ref, dk_ref, dv_ref, _, keep_ref, give_ref, total_ref):
    columns = dk_ref.shape[1]
    me = lax.axis_index("dp")
    core, my_x, my_y = me % 2, me // 2 // sides[1], me // 2 % sides[1]

    def slots(chip):
        x, y = chip // sides[1], chip % sides[1]
        ahead = (x - my_x + sides[0]) % sides[0]
        beside = (y - my_y + sides[1]) % sides[1]
        return ahead * sides[1] + beside, beside * sides[0] + ahead

    enc = enc_ref[...]
    total_ref[...] = dot_tn(enc, dk_ref[...])
    deal(core, total_ref, keep_ref, give_ref, slice(0, columns), slots)
    total_ref[...] = dot_tn(enc, dv_ref[...])
    deal(core, total_ref, keep_ref, give_ref, slice(columns, 2 * columns), slots)


def grads_kernel(*refs):
    normed_ref, act_ref, slope_ref, wout_ref, keep_ref, give_ref, total_ref = refs[8:]
    hidden = act_ref.shape[1]
    core = lax.axis_index("dp") % 2
    d_enc = join(refs[:8])
    total_ref[...] = dot_tn(d_enc, act_ref[...])
    deal(core, total_ref, keep_ref, give_ref, slice(0, hidden))
    d_pre = (dot_nt(d_enc, wout_ref[...]) * slope_ref[...].astype(F32)).astype(BF)
    total_ref[...] = dot_tn(normed_ref[...], d_pre)
    deal(core, total_ref, keep_ref, give_ref, slice(hidden, 2 * hidden))


def total_kernel(every_ref, first_ref, second_ref):
    total = every_ref[0].astype(F32)
    for chip in range(1, every_ref.shape[0]):
        total = total + every_ref[chip].astype(F32)
    rows, hidden = first_ref.shape
    first_ref[...] = total[:rows, :hidden]
    second_ref[...] = total[:rows, hidden:]


def swap_cores(give, devices):
    return lax.ppermute(give, "dp", [(i, i ^ 1) for i in range(devices)])


def scatter_chips(pair, devices):
    chips = devices // 2
    groups = [[chip * 2 + c for chip in range(chips)] for c in range(2)]
    return lax.all_to_all(pair, "dp", 0, 0, axis_index_groups=groups, tiled=True)


def scatter_axis(pieces, turn, sides, devices):
    total = pieces[0].astype(F32)
    for k in range(1, sides[0]):
        perm = []
        for i in range(devices):
            x, y, core = i // (2 * sides[1]), i // 2 % sides[1], i % 2
            if core == turn:
                x = (x + k) % sides[0]
            else:
                y = (y + k) % sides[1]
            perm.append((i, (x * sides[1] + y) * 2 + core))
        total = total + lax.ppermute(pieces[k], "dp", perm).astype(F32)
    return total


def scatter_across(keep, give, sides, devices):
    got = swap_cores(give, devices)
    across, beside = sides
    cut = (across, beside) + keep.shape[1:]
    keep, got = keep.reshape(cut), got.reshape(cut)
    pieces = [(keep[k].astype(F32) + got[k].astype(F32)).astype(BF) for k in range(across)]
    return scatter_axis(pieces, 0, sides, devices).astype(BF)


def per_device(queries, neighbours, targets, counts, in_weight, out_weight, kv_weight, d_context):
    length, holding, width = neighbours.shape
    owners = lax.axis_size("dp")
    ranks = lax.axis_size("mp")
    tokens = length // ranks
    token_rows, columns = queries.shape
    hidden = in_weight.shape[1]
    spans = token_rows // SPAN
    blocks = NEIGH * spans
    my_rank = lax.axis_index("mp")
    across = 1
    while across * across < owners // 2:
        across *= 2
    sides = (across, owners // 2 // across)
    piece = blocks * tokens
    rows = ranks * piece
    chips = owners // 2
    out_rows = width // owners
    pad_rows = -(-out_rows // 16) * 16

    own = lax.dynamic_slice_in_dim(neighbours, my_rank * tokens, tokens, 0).reshape(tokens * holding, width)
    is_live = jnp.arange(holding, dtype=jnp.int32) < counts[0]
    dest = jnp.where(is_live, targets // blocks, -1)
    place = targets % blocks
    marks = jnp.arange(PLACE, dtype=jnp.int32)[None, :] == jnp.tile(place, tokens)[:, None]
    payload = jnp.concatenate([own, marks.astype(BF)], axis=1)
    row_ids = jnp.arange(owners * tokens, dtype=jnp.int32)
    col_ids = jnp.arange(tokens * holding, dtype=jnp.int32)
    pick = jnp.logical_and(
        (row_ids // tokens)[:, None] == jnp.tile(dest, tokens)[None, :],
        (row_ids % tokens)[:, None] == (col_ids // holding)[None, :],
    ).astype(BF)
    sent = dot_nn(pick, payload).astype(BF).reshape(owners, tokens, width + PLACE)
    got = lax.all_to_all(sent, "dp", 0, 0, tiled=True).reshape(owners * tokens, width + PLACE)
    (raw,) = call(
        functools.partial(place_kernel, tokens, blocks),
        [shape_of((piece, width))],
        got,
        flops=2 * owners * tokens * piece * width,
    )
    normed, act, slope, *parts = call(
        encode_kernel,
        [
            shape_of((rows, width)),
            shape_of((rows, hidden)),
            shape_of((rows, hidden)),
            *part_shapes(piece, width),
        ],
        *gather_ring(raw, ranks),
        in_weight.T,
        out_weight,
        flops=4 * rows * width * hidden,
    )
    encoded, _ = scatter_ring(parts, ranks, raw)
    context, d_queries, enc, dk, dv, *parts = call(
        functools.partial(attend_kernel, spans, ranks),
        [
            shape_of((token_rows, columns)),
            shape_of((token_rows, columns)),
            shape_of((rows, width)),
            shape_of((rows, columns)),
            shape_of((rows, columns)),
            *part_shapes(piece, width),
        ],
        *gather_ring(encoded, ranks),
        kv_weight[:, 0, :],
        kv_weight[:, 1, :],
        queries,
        d_context,
        flops=8 * rows * width * columns,
    )

    def kv_grads(relayed):
        keep, give = call(
            functools.partial(kv_grads_kernel, sides),
            [shape_of((chips, pad_rows, 2 * columns))] * 2,
            enc,
            dk,
            dv,
            relayed,
            scratch=[pltpu.VMEM((width, columns), F32)],
            flops=4 * rows * width * columns,
            after=1,
        )
        return scatter_across(keep, give, sides, owners)

    d_encoded, half_kv = scatter_ring(parts, ranks, beside=kv_grads)
    keep, give = call(
        grads_kernel,
        [shape_of((chips, pad_rows, 2 * hidden))] * 2,
        *gather_ring(d_encoded, ranks),
        normed,
        act,
        slope,
        out_weight,
        scratch=[pltpu.VMEM((width, hidden), F32)],
        flops=6 * rows * width * hidden,
    )
    grad_kv = scatter_axis([half_kv[k] for k in range(sides[1])], 1, sides, owners)
    pair = (keep.astype(F32) + swap_cores(give, owners).astype(F32)).astype(BF)
    grad_out_t, grad_in = call(
        total_kernel, [shape_of((out_rows, hidden), F32)] * 2, scatter_chips(pair, owners)
    )
    return (
        context,
        d_queries,
        grad_kv[:out_rows].reshape(out_rows, 2, columns),
        grad_in,
        grad_out_t.T,
    )


def solution(mesh):
    placed = (
        P("dp", "mp"),
        P(None, "dp", None),
        P("dp"),
        P("dp"),
        P(None, "mp"),
        P("mp", None),
        P(None, None, "mp"),
        P("dp", "mp"),
    )
    return jax.shard_map(
        per_device,
        mesh=mesh,
        in_specs=placed,
        out_specs=(P("dp", "mp"), P("dp", "mp"), P("dp", None, "mp"), P("dp", "mp"), P("mp", "dp")),
        check_vma=False,
    )
```

```python
import functools

import jax
import jax.numpy as jnp
from jax import lax
from jax.experimental import pallas as pl
from jax.experimental.pallas import tpu as pltpu
from jax.sharding import PartitionSpec as P

DH = 128
SPAN = 64
NEIGH = 2
PLACE = 128
OFFSETS = (0, 1, 3, -1, -3, 2, -2, 4)
VMEM_LIMIT = 24 * 1024 * 1024

GELU_C = 0.7978845608028654
GELU_A = 0.044715
EPSILON = 1e-06

BF = jnp.bfloat16
F32 = jnp.float32


def dot_nn(a, b):
    return lax.dot_general(a, b, (((1,), (0,)), ((), ())), preferred_element_type=F32)


def dot_nt(a, b):
    return lax.dot_general(a, b, (((1,), (1,)), ((), ())), preferred_element_type=F32)


def dot_tn(a, b):
    return lax.dot_general(a, b, (((0,), (0,)), ((), ())), preferred_element_type=F32)


def call(kernel, outs, *args, scratch=(), flops=0, after=0, scalars=0):
    moved = sum(a.size * a.dtype.itemsize for a in args)
    moved += sum(o.size * o.dtype.itemsize for o in outs)
    whole = pl.BlockSpec(memory_space=pltpu.VMEM)
    unread = pl.BlockSpec(memory_space=pl.ANY)
    scalar = pl.BlockSpec(memory_space=pltpu.SMEM)
    return pl.pallas_call(
        kernel,
        out_shape=outs,
        in_specs=[scalar] * scalars + [whole] * (len(args) - scalars - after) + [unread] * after,
        out_specs=[whole] * len(outs),
        scratch_shapes=list(scratch),
        compiler_params=pltpu.CompilerParams(vmem_limit_bytes=VMEM_LIMIT),
        cost_estimate=pl.CostEstimate(flops=flops, bytes_accessed=moved, transcendentals=0),
    )(*args)


def shape_of(shape, dtype=BF):
    return jax.ShapeDtypeStruct(shape, dtype)


def send_kernel(tokens, blocks, targets_ref, counts_ref, own_ref, sent_ref):
    rows, holding = sent_ref.shape[0], targets_ref.shape[0]
    width = own_ref.shape[1]
    live = counts_ref[0]
    col = lax.broadcasted_iota(jnp.int32, (1, tokens * holding), 1)
    row = lax.broadcasted_iota(jnp.int32, (tokens * holding, 1), 0)
    dest = jnp.full(col.shape, -1, jnp.int32)
    place = jnp.zeros(row.shape, jnp.int32)
    for slot in range(holding):
        target = targets_ref[slot]
        owner = jnp.where(slot < live, target // blocks, -1)
        dest = jnp.where(col % holding == slot, owner, dest)
        place = jnp.where(row % holding == slot, target % blocks, place)
    marks = (lax.broadcasted_iota(jnp.int32, (tokens * holding, PLACE), 1) == place).astype(BF)
    out_row = lax.broadcasted_iota(jnp.int32, (rows, tokens * holding), 0)
    wanted = jnp.where(dest < 0, -1, dest * tokens + col // holding)
    pick = (out_row == wanted).astype(BF)
    sent_ref[:, :width] = dot_nn(pick, own_ref[...]).astype(BF)
    sent_ref[:, width:] = dot_nn(pick, marks).astype(BF)


def place_kernel(tokens, blocks, got_ref, raw_ref):
    rows, width = got_ref.shape
    wide = width - PLACE
    marks = got_ref[:, wide:]
    spread_rows = lax.broadcasted_iota(jnp.int32, (PLACE, blocks * tokens), 0)
    spread_cols = lax.broadcasted_iota(jnp.int32, (PLACE, blocks * tokens), 1)
    spread = (spread_rows == spread_cols // tokens).astype(BF)
    chosen = dot_nn(marks, spread)
    row_token = lax.broadcasted_iota(jnp.int32, chosen.shape, 0) % tokens
    col_token = lax.broadcasted_iota(jnp.int32, chosen.shape, 1) % tokens
    chosen = jnp.where(row_token == col_token, chosen, 0.0).astype(BF)
    raw_ref[...] = dot_tn(chosen, got_ref[:, :wide]).astype(BF)


def join(refs):
    return jnp.concatenate([r[...] for r in refs], axis=0)


def part_shapes(piece, width):
    return [shape_of((r * piece, width)) for r in (1, 2, 2, 1, 1, 1)]


def write_parts(part, refs):
    at = 0
    for ref in refs:
        rows = ref.shape[0]
        ref[...] = part[at : at + rows]
        at += rows


def on_first_core():
    return jnp.full((1, 1), lax.axis_index("dp") % 2) == 0


def pick_kernel(first_ref, second_ref, out_ref):
    out_ref[...] = jnp.where(on_first_core(), first_ref[...], second_ref[...])


def relay_kernel(ahead_ref, behind_ref, far_ref, p2_ref, m2_ref, p2_out, m2_out):
    piece = p2_ref.shape[0]
    far = far_ref[...].astype(F32)
    first = on_first_core()
    plus = p2_ref[...].astype(F32) + ahead_ref[piece:].astype(F32)
    minus = m2_ref[...].astype(F32) + behind_ref[piece:].astype(F32)
    p2_out[...] = (plus + jnp.where(first, far, 0.0)).astype(BF)
    m2_out[...] = (minus + jnp.where(first, 0.0, far)).astype(BF)


def sum_kernel(*refs):
    own_ref, ahead_ref, behind_ref, p2_ref, m2_ref = refs[:5]
    piece = own_ref.shape[0]
    total = own_ref[...].astype(F32) + ahead_ref[:piece].astype(F32) + behind_ref[:piece].astype(F32)
    total = total + p2_ref[...].astype(F32) + m2_ref[...].astype(F32)
    for extra in refs[5:-1]:
        total = total + extra[...].astype(F32)
    refs[-1][...] = total.astype(BF)


def shift(array, hops, ranks):
    return lax.ppermute(array, "mp", [(i, (i + hops) % ranks) for i in range(ranks)])


def shift_by_core(array, hops, ranks):
    perm = []
    for i in range(lax.axis_size("dp")):
        step = hops if i % 2 == 0 else -hops
        perm += [(i * ranks + j, i * ranks + (j + step) % ranks) for j in range(ranks)]
    return lax.ppermute(array, ("dp", "mp"), perm)


def gather_ring(piece, ranks):
    p2, m2 = shift(piece, -2, ranks), shift(piece, 2, ranks)
    p1, m1 = shift(piece, -1, ranks), shift(piece, 1, ranks)
    (far,) = call(pick_kernel, [shape_of(piece.shape)], p2, m2)
    far = shift_by_core(far, -2, ranks)
    p3, m3 = shift(p2, -1, ranks), shift(m2, 1, ranks)
    return (piece, p1, p3, m1, m3, p2, m2, far)


def scatter_ring(parts, ranks, *extra, beside=None):
    own, ahead, behind, p2, m2, far = parts
    far = shift_by_core(far, 2, ranks)
    ahead, behind = shift(ahead, 1, ranks), shift(behind, -1, ranks)
    p2, m2 = call(relay_kernel, [shape_of(p2.shape)] * 2, ahead, behind, far, p2, m2)
    kept = beside(p2) if beside else None
    p2, m2 = shift(p2, 2, ranks), shift(m2, -2, ranks)
    (total,) = call(sum_kernel, [shape_of(own.shape)], own, ahead, behind, p2, m2, *extra)
    return total, kept


def encode_kernel(*refs):
    win_ref, wout_ref, normed_ref, act_ref, slope_ref = refs[8:13]
    wide = join(refs[:8]).astype(F32)
    mean_square = jnp.mean(wide * wide, axis=-1, keepdims=True)
    normed = (wide * lax.rsqrt(mean_square + EPSILON)).astype(BF)
    normed_ref[...] = normed
    pre = dot_nt(normed, win_ref[...])
    square = pre * pre
    tanh_value = jnp.tanh(GELU_C * (pre + GELU_A * square * pre))
    act = (0.5 * pre * (1.0 + tanh_value)).astype(BF)
    act_ref[...] = act
    slope = 0.5 * (1.0 + tanh_value) + 0.5 * pre * (1.0 - tanh_value * tanh_value) * GELU_C * (
        1.0 + 3.0 * GELU_A * square
    )
    slope_ref[...] = slope.astype(BF)
    write_parts(dot_nn(act, wout_ref[...]).astype(BF), refs[13:])


def deal(core, total_ref, keep_ref, give_ref, cols, slots=None):
    chips = keep_ref.shape[0]
    rows = total_ref.shape[0] // (2 * chips)
    filler = jnp.zeros((keep_ref.shape[1] - rows, total_ref.shape[1]), BF)

    def write(refs):
        for chip in range(chips):
            for kind, ref in enumerate(refs):
                at = (2 * chip + kind) * rows
                slot = slots(chip)[kind] if slots else chip
                ref[slot, :rows, cols] = total_ref[at : at + rows, :].astype(BF)
                if filler.shape[0]:
                    ref[slot, rows:, cols] = filler

    @pl.when(core == 0)
    def _():
        write((keep_ref, give_ref))

    @pl.when(core != 0)
    def _():
        write((give_ref, keep_ref))


def attend_kernel(spans, ranks, *refs):
    kw_ref, vw_ref, q_ref, g_ref, ctx_ref, dq_ref, enc_ref, dk_ref, dv_ref = refs[8:17]
    scaling = DH ** (-0.5)
    enc = join(refs[:8])
    enc_ref[...] = enc
    rows, columns = dk_ref.shape
    piece = rows // ranks // spans
    cut = (ranks, spans, piece, columns)
    keys = dot_nn(enc, kw_ref[...]).astype(BF).reshape(cut)
    values = dot_nn(enc, vw_ref[...]).astype(BF).reshape(cut)
    for s in range(spans):
        q_rows = slice(s * SPAN, (s + 1) * SPAN)
        heads = [slice(h * DH, (h + 1) * DH) for h in range(columns // DH)]
        ks = [keys[:, s, :, cols].reshape(ranks * piece, DH) for cols in heads]
        vs = [values[:, s, :, cols].reshape(ranks * piece, DH) for cols in heads]
        qs = [q_ref[q_rows, cols] for cols in heads]
        gs = [g_ref[q_rows, cols] for cols in heads]
        scores = [dot_nt(q, k) * scaling for q, k in zip(qs, ks)]
        d_probs = [dot_nt(g, v) for g, v in zip(gs, vs)]
        wide = []
        for x in scores:
            weights = jnp.exp(x - jnp.max(x, axis=-1, keepdims=True))
            wide.append(weights / jnp.sum(weights, axis=-1, keepdims=True))
        probs = [x.astype(BF) for x in wide]
        d_scores = [
            (p * (d - jnp.sum(d * p, axis=-1, keepdims=True)) * scaling).astype(BF)
            for p, d in zip(wide, d_probs)
        ]
        for cols, p, d, k, v, q, g in zip(heads, probs, d_scores, ks, vs, qs, gs):
            ctx_ref[q_rows, cols] = dot_nn(p, v).astype(BF)
            dq_ref[q_rows, cols] = dot_nn(d, k).astype(BF)
            d_k = dot_tn(d, q).astype(BF)
            d_v = dot_tn(p, g).astype(BF)
            for r in range(ranks):
                at = (r * spans + s) * piece
                dk_ref[at : at + piece, cols] = d_k[r * piece : (r + 1) * piece]
                dv_ref[at : at + piece, cols] = d_v[r * piece : (r + 1) * piece]
    part = (dot_nt(dk_ref[...], kw_ref[...]) + dot_nt(dv_ref[...], vw_ref[...])).astype(BF)
    write_parts(part, refs[17:])


def kv_grads_kernel(sides, enc_ref, dk_ref, dv_ref, _, keep_ref, give_ref, total_ref):
    columns = dk_ref.shape[1]
    me = lax.axis_index("dp")
    core, my_x, my_y = me % 2, me // 2 // sides[1], me // 2 % sides[1]

    def slots(chip):
        x, y = chip // sides[1], chip % sides[1]
        ahead = (x - my_x + sides[0]) % sides[0]
        beside = (y - my_y + sides[1]) % sides[1]
        return ahead * sides[1] + beside, beside * sides[0] + ahead

    enc = enc_ref[...]
    total_ref[...] = dot_tn(enc, dk_ref[...])
    deal(core, total_ref, keep_ref, give_ref, slice(0, columns), slots)
    total_ref[...] = dot_tn(enc, dv_ref[...])
    deal(core, total_ref, keep_ref, give_ref, slice(columns, 2 * columns), slots)


def grads_kernel(*refs):
    normed_ref, act_ref, slope_ref, wout_ref, keep_ref, give_ref, total_ref = refs[8:]
    hidden = act_ref.shape[1]
    core = lax.axis_index("dp") % 2
    d_enc = join(refs[:8])
    total_ref[...] = dot_tn(d_enc, act_ref[...])
    deal(core, total_ref, keep_ref, give_ref, slice(0, hidden))
    d_pre = (dot_nt(d_enc, wout_ref[...]) * slope_ref[...].astype(F32)).astype(BF)
    total_ref[...] = dot_tn(normed_ref[...], d_pre)
    deal(core, total_ref, keep_ref, give_ref, slice(hidden, 2 * hidden))


def total_kernel(every_ref, first_ref, second_ref):
    total = every_ref[0].astype(F32)
    for chip in range(1, every_ref.shape[0]):
        total = total + every_ref[chip].astype(F32)
    rows, hidden = first_ref.shape
    first_ref[...] = total[:rows, :hidden]
    second_ref[...] = total[:rows, hidden:]


def swap_cores(give, devices):
    return lax.ppermute(give, "dp", [(i, i ^ 1) for i in range(devices)])


def scatter_chips(pair, devices):
    chips = devices // 2
    groups = [[chip * 2 + c for chip in range(chips)] for c in range(2)]
    return lax.all_to_all(pair, "dp", 0, 0, axis_index_groups=groups, tiled=True)


def scatter_axis(pieces, turn, sides, devices):
    total = pieces[0].astype(F32)
    for k in range(1, sides[0]):
        perm = []
        for i in range(devices):
            x, y, core = i // (2 * sides[1]), i // 2 % sides[1], i % 2
            if core == turn:
                x = (x + k) % sides[0]
            else:
                y = (y + k) % sides[1]
            perm.append((i, (x * sides[1] + y) * 2 + core))
        total = total + lax.ppermute(pieces[k], "dp", perm).astype(F32)
    return total


def scatter_across(keep, give, sides, devices):
    got = swap_cores(give, devices)
    across, beside = sides
    cut = (across, beside) + keep.shape[1:]
    keep, got = keep.reshape(cut), got.reshape(cut)
    pieces = [(keep[k].astype(F32) + got[k].astype(F32)).astype(BF) for k in range(across)]
    return scatter_axis(pieces, 0, sides, devices).astype(BF)


def per_device(queries, neighbours, targets, counts, in_weight, out_weight, kv_weight, d_context):
    length, holding, width = neighbours.shape
    owners = lax.axis_size("dp")
    ranks = lax.axis_size("mp")
    tokens = length // ranks
    token_rows, columns = queries.shape
    hidden = in_weight.shape[1]
    spans = token_rows // SPAN
    blocks = NEIGH * spans
    my_rank = lax.axis_index("mp")
    across = 1
    while across * across < owners // 2:
        across *= 2
    sides = (across, owners // 2 // across)
    piece = blocks * tokens
    rows = ranks * piece
    chips = owners // 2
    out_rows = width // owners
    pad_rows = -(-out_rows // 16) * 16

    own = lax.dynamic_slice_in_dim(neighbours, my_rank * tokens, tokens, 0).reshape(tokens * holding, width)
    (sent,) = call(
        functools.partial(send_kernel, tokens, blocks),
        [shape_of((owners * tokens, width + PLACE))],
        targets,
        counts,
        own,
        flops=2 * owners * tokens * tokens * holding * (width + PLACE),
        scalars=2,
    )
    sent = sent.reshape(owners, tokens, width + PLACE)
    got = lax.all_to_all(sent, "dp", 0, 0, tiled=True).reshape(owners * tokens, width + PLACE)
    (raw,) = call(
        functools.partial(place_kernel, tokens, blocks),
        [shape_of((piece, width))],
        got,
        flops=2 * owners * tokens * piece * width,
    )
    normed, act, slope, *parts = call(
        encode_kernel,
        [
            shape_of((rows, width)),
            shape_of((rows, hidden)),
            shape_of((rows, hidden)),
            *part_shapes(piece, width),
        ],
        *gather_ring(raw, ranks),
        in_weight.T,
        out_weight,
        flops=4 * rows * width * hidden,
    )
    encoded, _ = scatter_ring(parts, ranks, raw)
    context, d_queries, enc, dk, dv, *parts = call(
        functools.partial(attend_kernel, spans, ranks),
        [
            shape_of((token_rows, columns)),
            shape_of((token_rows, columns)),
            shape_of((rows, width)),
            shape_of((rows, columns)),
            shape_of((rows, columns)),
            *part_shapes(piece, width),
        ],
        *gather_ring(encoded, ranks),
        kv_weight[:, 0, :],
        kv_weight[:, 1, :],
        queries,
        d_context,
        flops=8 * rows * width * columns,
    )

    def kv_grads(relayed):
        keep, give = call(
            functools.partial(kv_grads_kernel, sides),
            [shape_of((chips, pad_rows, 2 * columns))] * 2,
            enc,
            dk,
            dv,
            relayed,
            scratch=[pltpu.VMEM((width, columns), F32)],
            flops=4 * rows * width * columns,
            after=1,
        )
        return scatter_across(keep, give, sides, owners)

    d_encoded, half_kv = scatter_ring(parts, ranks, beside=kv_grads)
    keep, give = call(
        grads_kernel,
        [shape_of((chips, pad_rows, 2 * hidden))] * 2,
        *gather_ring(d_encoded, ranks),
        normed,
        act,
        slope,
        out_weight,
        scratch=[pltpu.VMEM((width, hidden), F32)],
        flops=6 * rows * width * hidden,
    )
    grad_kv = scatter_axis([half_kv[k] for k in range(sides[1])], 1, sides, owners)
    pair = (keep.astype(F32) + swap_cores(give, owners).astype(F32)).astype(BF)
    grad_out_t, grad_in = call(
        total_kernel, [shape_of((out_rows, hidden), F32)] * 2, scatter_chips(pair, owners)
    )
    return (
        context,
        d_queries,
        grad_kv[:out_rows].reshape(out_rows, 2, columns),
        grad_in,
        grad_out_t.T,
    )


def solution(mesh):
    placed = (
        P("dp", "mp"),
        P(None, "dp", None),
        P("dp"),
        P("dp"),
        P(None, "mp"),
        P("mp", None),
        P(None, None, "mp"),
        P("dp", "mp"),
    )
    return jax.shard_map(
        per_device,
        mesh=mesh,
        in_specs=placed,
        out_specs=(P("dp", "mp"), P("dp", "mp"), P("dp", None, "mp"), P("dp", "mp"), P("mp", "dp")),
        check_vma=False,
    )
```
